128 devices in a mesh: member: 64 (over z, y, x), region: 2 (over core).
Axes of the slice: x: 4, y: 4, z: 4, core: 2. Of those that a mesh axis runs over, the one named last changes fastest.
Arguments:
- prior_samples: float32 [1024, 64, 2, 1024], P('member', None, 'region'), may hold values from -6 to 6
- measured_point: int32 [64, 2, 256], P('member', 'region'), may hold values from 0 to 1023
- measured_reading: float32 [64, 2, 256], P('member', 'region'), may hold values from -6 to 6
- measurement_noise: bfloat16 [64, 2, 256, 1024], P('member', 'region'), may hold values from -6 to 6
- noise_kind: int32 [64, 2], P('member'), may hold values from 0 to 3
- taper_set: int32 [64, 2], P('member'), may hold values from 0 to 1, as said below
Outputs:
- increment: float32 [1024, 64, 2, 1024], P('member', None, 'region')
The draws below stay inside these ranges and needn't reach their ends.
Inputs may be any that keep to these rules, and one draw needn't show every extreme that they name: `taper_set`: along the 2 regions of a band the labels never fall, so that equal labels form runs of neighbouring regions; each label is the index of the first region of its run; in at least one band all regions form a single run.
All inputs are finite; a program needn't handle non-finite values.
Results may differ from the reference program's by a relative error of at most 0.0076.
Values may be sent and summed in bfloat16 or wider, within the bound.
No kernel may reach another device: no remote copies, remote signals or barrier semaphores. Data moves between devices by JAX's collectives and lax.ppermute only.
A program may use at most 64 MiB of HBM per device.

```python
import jax
import jax.numpy as jnp
from jax import lax

SAMPLE_TOTAL = 1024
POINTS_PER_ZONE = 1024
OBS = 256
ITERS = 4
MESH_STRIPES = 64
ZONES_PER_STRIPE = 2


def draw_taper_set(key, part):
    key = jax.random.fold_in(key, 7)
    break_key, band_key = jax.random.split(key)
    chosen = jax.random.randint(break_key, (MESH_STRIPES, ZONES_PER_STRIPE - 1), 0, 3)
    joined_band = jax.random.randint(band_key, (), 0, MESH_STRIPES)
    bands = jnp.arange(MESH_STRIPES, dtype=jnp.int32)[:, None]
    breaks = (chosen == 0).astype(jnp.int32)
    breaks = jnp.where(bands == joined_band, jnp.int32(0), breaks).astype(jnp.int32)
    leading = jnp.ones((MESH_STRIPES, 1), jnp.int32)
    flags = jnp.concatenate([leading, breaks], axis=1).astype(jnp.int32)
    places = jnp.arange(ZONES_PER_STRIPE, dtype=jnp.int32)[None, :]
    starts = jnp.where(flags == 1, places, jnp.int32(0)).astype(jnp.int32)
    return lax.cummax(starts, axis=1).astype(jnp.int32)


def place_ends(entries, stream_key, least, largest):
    dims = entries.shape
    index_at = [jax.random.randint(jax.random.fold_in(stream_key, axis), (), 0, dims[axis]) for axis in range(len(dims))]
    entries = entries.at[tuple(index_at)].set(least)
    longest = dims.index(max(dims))
    index_at[longest] = (index_at[longest] + 1) % dims[longest]
    return entries.at[tuple(index_at)].set(largest)


def levels(key, dims, cuts, least, largest):
    level, own = 1.0, jax.random.fold_in(key, 6)
    for position, shards_of in cuts:
        steps = jnp.exp(jax.random.uniform(jax.random.fold_in(own, position), (shards_of,), jnp.float32, least / len(cuts), largest / len(cuts)))
        level = level * jnp.repeat(steps, dims[position] // shards_of).reshape([-1 if axis == position else 1 for axis in range(len(dims))])
    return level


def centred(key, shape, scale, reach, shards=(), held_as=jnp.bfloat16):
    values = jax.random.normal(key, shape, jnp.float32) * scale
    if len(shards) > 0:
        values = levels(key, shape, shards, -0.22, 0.18) * values
    return jnp.clip(values, min=-reach, max=reach).astype(held_as)


def setup_inputs(seed: int = 0) -> dict:
    splits = jax.random.split(jax.random.key(seed), 7)
    prior_samples = centred(splits[0], (SAMPLE_TOTAL, MESH_STRIPES, ZONES_PER_STRIPE, POINTS_PER_ZONE), 1.0, 6.0, ((0, 64), (2, 2)), jnp.float32)
    measured_point = place_ends(jax.random.randint(splits[1], (MESH_STRIPES, ZONES_PER_STRIPE, OBS), 0, POINTS_PER_ZONE), jax.random.fold_in(splits[1], 1), 0, POINTS_PER_ZONE - 1).astype(jnp.int32)
    measured_reading = centred(splits[2], (MESH_STRIPES, ZONES_PER_STRIPE, OBS), 1.0, 6.0, ((0, 64), (1, 2)), jnp.float32)
    measurement_noise = centred(splits[3], (MESH_STRIPES, ZONES_PER_STRIPE, OBS, SAMPLE_TOTAL), 1.0, 6.0, ((0, 64), (1, 2)))
    noise_kind = place_ends(jax.random.randint(splits[4], (MESH_STRIPES, ZONES_PER_STRIPE), 0, 4), jax.random.fold_in(splits[4], 1), 0, 3).astype(jnp.int32)
    taper_set = draw_taper_set(jax.random.fold_in(splits[6], 71), 0)
    return dict(prior_samples=prior_samples, measured_point=measured_point, measured_reading=measured_reading, measurement_noise=measurement_noise, noise_kind=noise_kind, taper_set=taper_set)


taper_base = 0.7

def region_weights(groups):
    count = groups.shape[0]
    places = jnp.arange(count, dtype=jnp.int32)
    distance = jnp.abs(places[:, None] - places[None, :]).astype(jnp.float32)
    kept = groups[:, None] == groups[None, :]
    return jnp.where(kept, jnp.power(jnp.float32(taper_base), distance), jnp.float32(0.0))

def chebyshev(innovation, apply_operator, lowest, highest):
    center = 0.5 * (highest + lowest)
    radius = 0.5 * (highest - lowest)
    sigma_value = center / radius
    rho_value = 1.0 / sigma_value
    residual = innovation
    direction = residual / center
    solution = jnp.zeros_like(innovation)
    for sweep_index in range(ITERS):
        solution = solution + direction
        if sweep_index + 1 < ITERS:
            residual = residual - apply_operator(direction)
            rho_next = 1.0 / (2.0 * sigma_value - rho_value)
            direction = rho_next * rho_value * direction + 2.0 * rho_next / radius * residual
            rho_value = rho_next
    return solution

def lone_stripe(stripe_prior, stripe_points, stripe_readings, stripe_noise_draws, stripe_noise_kinds, stripe_taper_sets):
    sample_fields = stripe_prior.shape[0]
    sample_mean_state = lax.optimization_barrier(jnp.mean(stripe_prior, axis=0))
    sample_deviation = (stripe_prior - sample_mean_state).astype(jnp.bfloat16)
    measured_fields = jnp.take_along_axis(stripe_prior, stripe_points[None, :, :], axis=2)
    observed_mean = jnp.take_along_axis(sample_mean_state, stripe_points, axis=1)
    observed_rows = jnp.transpose(measured_fields, (1, 2, 0)).reshape(-1, sample_fields)
    obs_rows = jnp.transpose(measured_fields - observed_mean[None], (1, 2, 0)).reshape(-1, sample_fields).astype(jnp.bfloat16)
    variance = 0.5 * jnp.exp2(stripe_noise_kinds.astype(jnp.float32))
    row_variance = jnp.repeat(variance, OBS)
    innovation = stripe_readings.reshape(-1)[:, None] + jnp.sqrt(row_variance)[:, None] * stripe_noise_draws.reshape(-1, sample_fields).astype(jnp.float32) - observed_rows
    weights = region_weights(stripe_taper_sets)
    full_weights = jnp.repeat(jnp.repeat(weights, OBS, axis=0), OBS, axis=1)
    products = jnp.dot(obs_rows, obs_rows.T, preferred_element_type=jnp.float32)
    covariance = (full_weights * products / (sample_fields - 1)).astype(jnp.bfloat16)
    upper = row_variance + lax.optimization_barrier(jnp.sum(jnp.abs(covariance.astype(jnp.float32)), axis=1))
    lowest = 0.5 * jnp.exp2(jnp.min(stripe_noise_kinds).astype(jnp.float32))
    highest = lowest + jnp.max(upper)

    def apply_operator(direction):
        return row_variance[:, None] * direction + jnp.dot(covariance, direction.astype(jnp.bfloat16), preferred_element_type=jnp.float32)
    solution = chebyshev(innovation, apply_operator, lowest, highest).astype(jnp.bfloat16)
    cross = jnp.einsum('mrc,om->rco', sample_deviation.astype(jnp.float32), obs_rows.astype(jnp.float32), precision=lax.Precision.HIGHEST)
    region_rows = jnp.repeat(weights, OBS, axis=1)
    gain = (region_rows[:, None, :] * cross / (sample_fields - 1)).astype(jnp.bfloat16)
    return jnp.einsum('rco,om->mrc', gain.astype(jnp.float32), solution.astype(jnp.float32), precision=lax.Precision.HIGHEST)

def band_step(items):
    return lone_stripe(items[0], items[1], items[2], items[3], items[4], items[5])

def reference(prior_samples, measured_point, measured_reading, measurement_noise, noise_kind, taper_set):
    former_stripes = jnp.transpose(prior_samples, (1, 0, 2, 3))
    result = lax.map(band_step, (former_stripes, measured_point, measured_reading, measurement_noise, noise_kind, taper_set))
    return jnp.transpose(result, (1, 0, 2, 3))
```

```python
import jax
import jax.numpy as jnp
from jax import lax
from jax.experimental import pallas as pl
from jax.experimental.pallas import tpu as pltpu
from jax.sharding import PartitionSpec as P

ITERS = 4
TAPER_BASE = 0.7
LANES = 128
BANDS_PER_STEP = 8
VMEM = 56 * 1024 * 1024

f32 = jnp.float32
bf16 = jnp.bfloat16


def split3(value):
    high = value.astype(bf16)
    rest = value - high.astype(f32)
    middle = rest.astype(bf16)
    low = (rest - middle.astype(f32)).astype(bf16)
    return high, middle, low


def pack_members(x_ref, out_ref):
    members, bands, chunks, lanes = x_ref.shape
    cells = chunks * lanes
    flat = x_ref.reshape(members * bands * chunks, lanes)

    for band in range(bands):
        mean = jnp.sum(x_ref[:, band], axis=0) * (1.0 / members)
        high = mean.astype(bf16)
        low = (mean - high.astype(f32)).astype(bf16)
        held = high.astype(f32) + low.astype(f32)
        out_ref[band, :, cells : cells + lanes] = jnp.concatenate([high, low], axis=0)
        for chunk in range(chunks):
            rows = flat[pl.ds(band * chunks + chunk, members, stride=bands * chunks), :]
            out_ref[band, :, chunk * lanes : (chunk + 1) * lanes] = (
                rows - held[chunk : chunk + 1, :]
            ).astype(bf16)


def unpack_members(x_ref, out_ref):
    bands, members, cells = x_ref.shape
    chunks = cells // LANES
    flat = out_ref.reshape(members * bands * chunks, LANES)
    for band in range(bands):
        for chunk in range(chunks):
            flat[pl.ds(band * chunks + chunk, members, stride=bands * chunks), :] = x_ref[
                band, :, chunk * LANES : (chunk + 1) * LANES
            ].astype(f32)


def observe(x_ref, points_ref, readings_ref, anomaly_ref, seen_ref, means, spread, hot):
    sources, members, width = x_ref.shape
    cells = anomaly_ref.shape[1]
    total_members = anomaly_ref.shape[0]
    chunks = cells // LANES
    obs = points_ref.shape[1]

    for source in range(sources):
        tail = x_ref[source, :, cells:width].astype(f32)
        means[source] = tail[:chunks] + tail[chunks:]
    average = jnp.sum(means[...], axis=0) * (1.0 / sources)

    points = jnp.transpose(jnp.broadcast_to(points_ref[...], (LANES, obs)))
    lane = lax.broadcasted_iota(jnp.int32, (obs, LANES), 1)
    picked = jnp.zeros((obs, LANES), f32)
    for chunk in range(chunks):
        here = points == lane + chunk * LANES
        hot[:, chunk * LANES : (chunk + 1) * LANES] = jnp.where(here, 1.0, 0.0).astype(bf16)
        picked = picked + jnp.where(here, average[chunk : chunk + 1, :], 0.0)
    readings = jnp.transpose(jnp.broadcast_to(readings_ref[...], (LANES, obs)))
    base = readings - jnp.sum(picked, axis=1, keepdims=True)
    high, middle, low = split3(base)
    seen_ref[:, total_members : total_members + LANES] = jnp.where(
        lane == 0, high.astype(f32), jnp.where(lane == 1, middle.astype(f32), low.astype(f32))
    ).astype(bf16)

    spread[...] = means[...] - average[None]

    per_block = 16

    @pl.loop(0, sources // per_block)
    def _(block):
        for inner in range(per_block):
            source = block * per_block + inner
            rows = pl.ds(pl.multiple_of(source * members, members), members)
            shift = spread[source]
            for chunk in range(chunks):
                columns = slice(chunk * LANES, (chunk + 1) * LANES)
                anomaly_ref[rows, columns] = (
                    x_ref[source, :, columns].astype(f32) + shift[chunk : chunk + 1, :]
                ).astype(bf16)
        size = per_block * members
        span = pl.ds(pl.multiple_of(block * size, size), size)
        seen_ref[:, span] = lax.dot_general(
            hot[...],
            anomaly_ref[span, :],
            (((1,), (1,)), ((), ())),
            preferred_element_type=f32,
        ).astype(bf16)


def analyse(
    kinds_ref,
    groups_ref,
    anomaly_ref,
    own_ref,
    other_ref,
    own_noise_ref,
    other_noise_ref,
    out_ref,
    seen,
    covariance,
    gain,
    solved,
    residual,
    direction,
    tally,
):
    total_members, cells = anomaly_ref.shape
    tile = own_ref.shape[0]
    rows = 2 * tile
    region = lax.axis_index("region")
    own_kind = kinds_ref[0, region]
    other_kind = kinds_ref[0, 1 - region]
    one = jnp.int32(1)
    own_variance = 0.5 * lax.shift_left(one, own_kind).astype(f32)
    other_variance = 0.5 * lax.shift_left(one, other_kind).astype(f32)
    cross_weight = jnp.where(groups_ref[0, 0] == groups_ref[0, 1], f32(TAPER_BASE), f32(0.0))
    count = total_members - 1

    seen[:tile, :] = own_ref[:, :total_members]
    seen[tile:, :] = other_ref[:, :total_members]
    in_own = lax.broadcasted_iota(jnp.int32, (rows, 1), 0) < tile
    variance = jnp.where(in_own, own_variance, other_variance)
    weight_rows = jnp.where(in_own, f32(1.0), cross_weight)

    largest = f32(0.0)
    for half in range(2):
        block = seen[half * tile : (half + 1) * tile, :]
        product = lax.dot_general(
            seen[...], block, (((1,), (1,)), ((), ())), preferred_element_type=f32
        )
        weight = jnp.where(in_own == (half == 0), f32(1.0), cross_weight)
        covariance[:, half * tile : (half + 1) * tile] = (weight * product / count).astype(bf16)
    bound = variance + jnp.sum(jnp.abs(covariance[...].astype(f32)), axis=1, keepdims=True)
    largest = jnp.max(bound)
    lowest = jnp.minimum(own_variance, other_variance)
    highest = lowest + largest
    center = 0.5 * (highest + lowest)
    radius = 0.5 * (highest - lowest)
    sigma = center / radius
    rho = 1.0 / sigma

    own_base = jnp.sum(own_ref[:, total_members:].astype(f32)[:, :3], axis=1, keepdims=True)
    other_base = jnp.sum(other_ref[:, total_members:].astype(f32)[:, :3], axis=1, keepdims=True)
    own_scale = jnp.sqrt(jnp.full((1, 1), own_variance, f32))
    other_scale = jnp.sqrt(jnp.full((1, 1), other_variance, f32))
    width = residual.shape[1]

    steps = []
    for _ in range(ITERS - 1):
        rho_next = 1.0 / (2.0 * sigma - rho)
        steps.append((rho_next * rho, 2.0 * rho_next / radius))
        rho = rho_next

    @pl.loop(0, total_members // width)
    def _(block):
        span = pl.ds(pl.multiple_of(block * width, width), width)
        residual[:tile, :] = (
            own_base + own_scale * own_noise_ref[:, span].astype(f32) - own_ref[:, span].astype(f32)
        )
        residual[tile:, :] = (
            other_base
            + other_scale * other_noise_ref[:, span].astype(f32)
            - other_ref[:, span].astype(f32)
        )
        first = residual[...] / center
        direction[...] = first
        tally[...] = first
        for index, (keep, add) in enumerate(steps):
            now = direction[...]
            applied = variance * now + jnp.dot(
                covariance[...], now.astype(bf16), preferred_element_type=f32
            )
            left = residual[...] - applied
            later = keep * now + add * left
            if index < len(steps) - 1:
                residual[...] = left
                direction[...] = later
                tally[...] = tally[...] + later
            else:
                solved[:, span] = (tally[...] + later).astype(bf16)

    step = 256

    @pl.loop(0, cells // step)
    def _(block):
        span = pl.ds(pl.multiple_of(block * step, step), step)
        cross = jnp.dot(seen[...], anomaly_ref[:, span], preferred_element_type=f32)
        gain[:, span] = (weight_rows * cross / count).astype(bf16)

    @pl.loop(0, total_members // step)
    def _(block):
        span = pl.ds(pl.multiple_of(block * step, step), step)
        out_ref[span, :] = lax.dot_general(
            solved[:, span], gain[...], (((0,), (0,)), ((), ())), preferred_element_type=f32
        ).astype(bf16)


def whole(shape):
    return pl.BlockSpec(shape, lambda *_: (0,) * len(shape), memory_space=pltpu.VMEM)


def shards(
    prior_samples, measured_point, measured_reading, measurement_noise, noise_kind, taper_set
):
    members, bands, _, cells = prior_samples.shape
    tile = measured_point.shape[2]
    total = measurement_noise.shape[3]
    chunks = cells // LANES
    width = cells + LANES
    swap = [(0, 1), (1, 0)]

    own_noise = measurement_noise.reshape(tile, total)
    other_noise = lax.ppermute(own_noise, "region", swap)

    packed = pl.pallas_call(
        pack_members,
        grid=(bands // BANDS_PER_STEP,),
        in_specs=[
            pl.BlockSpec((members, BANDS_PER_STEP, chunks, LANES), lambda i: (0, i, 0, 0))
        ],
        out_specs=pl.BlockSpec((BANDS_PER_STEP, members, width), lambda i: (i, 0, 0)),
        out_shape=jax.ShapeDtypeStruct((bands, members, width), bf16),
        name="pack_members",
    )(prior_samples.reshape(members, bands, chunks, LANES))

    arrived = lax.all_to_all(packed, "member", split_axis=0, concat_axis=0, tiled=True)

    anomaly, seen = pl.pallas_call(
        observe,
        in_specs=[pl.BlockSpec(memory_space=pltpu.VMEM)] * 3,
        out_specs=[pl.BlockSpec(memory_space=pltpu.VMEM)] * 2,
        out_shape=[
            jax.ShapeDtypeStruct((total, cells), bf16),
            jax.ShapeDtypeStruct((tile, total + LANES), bf16),
        ],
        scratch_shapes=[
            pltpu.VMEM((bands, chunks, LANES), f32),
            pltpu.VMEM((bands, chunks, LANES), f32),
            pltpu.VMEM((tile, cells), bf16),
        ],
        compiler_params=pltpu.CompilerParams(vmem_limit_bytes=VMEM),
        name="observe",
    )(arrived, measured_point.reshape(1, tile), measured_reading.reshape(1, tile))

    other_seen = lax.ppermute(seen, "region", swap)

    increment = pl.pallas_call(
        analyse,
        in_specs=[pl.BlockSpec(memory_space=pltpu.SMEM)] * 2
        + [pl.BlockSpec(memory_space=pltpu.VMEM)] * 5,
        out_specs=pl.BlockSpec(memory_space=pltpu.VMEM),
        out_shape=jax.ShapeDtypeStruct((total, cells), bf16),
        scratch_shapes=[
            pltpu.VMEM((2 * tile, total), bf16),
            pltpu.VMEM((2 * tile, 2 * tile), bf16),
            pltpu.VMEM((2 * tile, cells), bf16),
            pltpu.VMEM((2 * tile, total), bf16),
            pltpu.VMEM((2 * tile, 256), f32),
            pltpu.VMEM((2 * tile, 256), f32),
            pltpu.VMEM((2 * tile, 256), f32),
        ],
        compiler_params=pltpu.CompilerParams(vmem_limit_bytes=VMEM),
        name="analyse",
    )(noise_kind, taper_set, anomaly, seen, other_seen, own_noise, other_noise)

    returned = lax.all_to_all(
        increment.reshape(bands, members, cells), "member", split_axis=0, concat_axis=0, tiled=True
    )

    unpacked = pl.pallas_call(
        unpack_members,
        grid=(bands // BANDS_PER_STEP,),
        in_specs=[pl.BlockSpec((BANDS_PER_STEP, members, cells), lambda i: (i, 0, 0))],
        out_specs=pl.BlockSpec((members, BANDS_PER_STEP, chunks, LANES), lambda i: (0, i, 0, 0)),
        out_shape=jax.ShapeDtypeStruct((members, bands, chunks, LANES), f32),
        name="unpack_members",
    )(returned)
    return unpacked.reshape(members, bands, 1, cells)


def solution(mesh):
    return jax.shard_map(
        shards,
        mesh=mesh,
        in_specs=(
            P("member", None, "region", None),
            P("member", "region", None),
            P("member", "region", None),
            P("member", "region", None, None),
            P("member", None),
            P("member", None),
        ),
        out_specs=P("member", None, "region", None),
        check_vma=False,
    )
```

```python
import jax
import jax.numpy as jnp
from jax import lax
from jax.experimental import pallas as pl
from jax.experimental.pallas import tpu as pltpu
from jax.sharding import PartitionSpec as P

ITERS = 4
TAPER_BASE = 0.7
LANES = 128
BANDS_PER_STEP = 8
MIB = 1024 * 1024

f32 = jnp.float32
bf16 = jnp.bfloat16


def split3(value):
    high = value.astype(bf16)
    rest = value - high.astype(f32)
    middle = rest.astype(bf16)
    low = (rest - middle.astype(f32)).astype(bf16)
    return high, middle, low


def row_order(rows, members, chunks):
    to = lax.broadcasted_iota(jnp.int32, (rows, rows), 0)
    source = lax.broadcasted_iota(jnp.int32, (rows, rows), 1)
    wanted = lax.rem(to, members) * chunks + lax.div(to, members)
    return jnp.where(source == wanted, 1.0, 0.0).astype(bf16)


def pack_members(x_ref, out_ref):
    members, bands, chunks, lanes = x_ref.shape
    cells = chunks * lanes
    rows = members * chunks
    order = row_order(rows, members, chunks)
    for pair in range(bands // 2):
        parts = []
        for band in (2 * pair, 2 * pair + 1):
            values = x_ref[:, band]
            mean = jnp.sum(values, axis=0) * (1.0 / members)
            high = mean.astype(bf16)
            low = (mean - high.astype(f32)).astype(bf16)
            held = high.astype(f32) + low.astype(f32)
            out_ref[band, :, cells : cells + lanes] = jnp.concatenate([high, low], axis=0)
            parts.append((values - held[None]).reshape(rows, lanes).astype(bf16))
        moved = jnp.dot(
            order, jnp.concatenate(parts, axis=1), preferred_element_type=f32
        ).astype(bf16)
        for index in range(2):
            for chunk in range(chunks):
                out_ref[2 * pair + index, :, chunk * lanes : (chunk + 1) * lanes] = moved[
                    chunk * members : (chunk + 1) * members, index * lanes : (index + 1) * lanes
                ]


def unpack_members(x_ref, out_ref):
    bands, members, cells = x_ref.shape
    chunks = cells // LANES
    rows = members * chunks
    order = row_order(rows, chunks, members)
    for pair in range(bands // 2):
        parts = []
        for band in (2 * pair, 2 * pair + 1):
            parts.append(
                jnp.concatenate(
                    [x_ref[band, :, c * LANES : (c + 1) * LANES] for c in range(chunks)], axis=0
                )
            )
        moved = jnp.dot(order, jnp.concatenate(parts, axis=1), preferred_element_type=f32)
        for index in range(2):
            out_ref[:, 2 * pair + index] = moved[
                :, index * LANES : (index + 1) * LANES
            ].reshape(members, chunks, LANES)


def observe(x_ref, points_ref, readings_ref, anomaly_ref, seen_ref, means, spread, hot):
    sources, members, width = x_ref.shape
    cells = anomaly_ref.shape[1]
    total_members = anomaly_ref.shape[0]
    chunks = cells // LANES
    obs = points_ref.shape[1]

    for source in range(sources):
        tail = x_ref[source, :, cells:width].astype(f32)
        means[source] = tail[:chunks] + tail[chunks:]
    average = jnp.sum(means[...], axis=0) * (1.0 / sources)

    points = jnp.transpose(jnp.broadcast_to(points_ref[...], (LANES, obs)))
    lane = lax.broadcasted_iota(jnp.int32, (obs, LANES), 1)
    picked = jnp.zeros((obs, LANES), f32)
    for chunk in range(chunks):
        here = points == lane + chunk * LANES
        hot[:, chunk * LANES : (chunk + 1) * LANES] = jnp.where(here, 1.0, 0.0).astype(bf16)
        picked = picked + jnp.where(here, average[chunk : chunk + 1, :], 0.0)
    readings = jnp.transpose(jnp.broadcast_to(readings_ref[...], (LANES, obs)))
    base = readings - jnp.sum(picked, axis=1, keepdims=True)
    high, middle, low = split3(base)
    seen_ref[:, total_members : total_members + LANES] = jnp.where(
        lane == 0, high.astype(f32), jnp.where(lane == 1, middle.astype(f32), low.astype(f32))
    ).astype(bf16)

    spread[...] = means[...] - average[None]

    per_block = 16

    @pl.loop(0, sources // per_block)
    def _(block):
        for inner in range(per_block):
            source = block * per_block + inner
            rows = pl.ds(pl.multiple_of(source * members, members), members)
            shift = spread[source]
            for chunk in range(chunks):
                columns = slice(chunk * LANES, (chunk + 1) * LANES)
                anomaly_ref[rows, columns] = (
                    x_ref[source, :, columns].astype(f32) + shift[chunk : chunk + 1, :]
                ).astype(bf16)
        size = per_block * members
        span = pl.ds(pl.multiple_of(block * size, size), size)
        seen_ref[:, span] = lax.dot_general(
            hot[...],
            anomaly_ref[span, :],
            (((1,), (1,)), ((), ())),
            preferred_element_type=f32,
        ).astype(bf16)


def analyse(
    kinds_ref,
    groups_ref,
    anomaly_ref,
    own_ref,
    other_ref,
    own_noise_ref,
    other_noise_ref,
    out_ref,
    seen,
    covariance,
    gain,
    solved,
    zero,
    one_step,
    two_steps,
):
    total_members, cells = anomaly_ref.shape
    tile = own_ref.shape[0]
    rows = 2 * tile
    region = lax.axis_index("region")
    own_kind = kinds_ref[0, region]
    other_kind = kinds_ref[0, 1 - region]
    one = jnp.int32(1)
    own_variance = 0.5 * lax.shift_left(one, own_kind).astype(f32)
    other_variance = 0.5 * lax.shift_left(one, other_kind).astype(f32)
    cross_weight = jnp.where(groups_ref[0, 0] == groups_ref[0, 1], f32(TAPER_BASE), f32(0.0))
    count = total_members - 1

    seen[:tile, :] = own_ref[:, :total_members]
    seen[tile:, :] = other_ref[:, :total_members]
    in_own = lax.broadcasted_iota(jnp.int32, (rows, 1), 0) < tile
    variance = jnp.where(in_own, own_variance, other_variance)
    weight_rows = jnp.where(in_own, f32(1.0), cross_weight)

    for half in range(2):
        block = seen[half * tile : (half + 1) * tile, :]
        product = lax.dot_general(
            seen[...], block, (((1,), (1,)), ((), ())), preferred_element_type=f32
        )
        weight = jnp.where(in_own == (half == 0), f32(1.0), cross_weight)
        covariance[:, half * tile : (half + 1) * tile] = (product * (weight / count)).astype(bf16)
    bound = variance + jnp.sum(jnp.abs(covariance[...].astype(f32)), axis=1, keepdims=True)
    largest = jnp.max(bound)
    lowest = jnp.minimum(own_variance, other_variance)
    highest = lowest + largest
    center = 0.5 * (highest + lowest)
    radius = 0.5 * (highest - lowest)
    sigma = center / radius
    rho = 1.0 / sigma

    own_base = jnp.sum(own_ref[:, total_members:].astype(f32)[:, :3], axis=1, keepdims=True)
    other_base = jnp.sum(other_ref[:, total_members:].astype(f32)[:, :3], axis=1, keepdims=True)
    own_scale = jnp.sqrt(jnp.full((1, 1), own_variance, f32))
    other_scale = jnp.sqrt(jnp.full((1, 1), other_variance, f32))
    width = zero.shape[1]

    steps = []
    reach_before, keep_before = 1.0 / center, f32(0.0)
    for _ in range(ITERS - 1):
        rho_next = 1.0 / (2.0 * sigma - rho)
        keep = rho_next * rho
        reach = 2.0 * rho_next / radius
        ratio = reach / reach_before
        steps.append((keep + ratio - reach * variance, ratio * keep_before, reach))
        rho, reach_before, keep_before = rho_next, reach, keep
    inverse = 1.0 / center

    @pl.loop(0, total_members // width)
    def _(block):
        span = pl.ds(pl.multiple_of(block * width, width), width)
        zero[:tile, :] = inverse * (
            own_base + own_scale * own_noise_ref[:, span].astype(f32) - own_ref[:, span].astype(f32)
        )
        zero[tile:, :] = inverse * (
            other_base
            + other_scale * other_noise_ref[:, span].astype(f32)
            - other_ref[:, span].astype(f32)
        )
        ahead, _, reach = steps[0]
        now = zero[...]
        one_step[...] = ahead * now - reach * jnp.dot(
            covariance[...], now.astype(bf16), preferred_element_type=f32
        )
        ahead, back, reach = steps[1]
        now = one_step[...]
        two_steps[...] = (
            ahead * now
            - back * zero[...]
            - reach * jnp.dot(covariance[...], now.astype(bf16), preferred_element_type=f32)
        )
        ahead, back, reach = steps[2]
        now = two_steps[...]
        solved[:, span] = (
            (1.0 + ahead) * now
            + (1.0 - back) * one_step[...]
            + zero[...]
            - reach * jnp.dot(covariance[...], now.astype(bf16), preferred_element_type=f32)
        ).astype(bf16)

    step = 256

    @pl.loop(0, cells // step)
    def _(block):
        span = pl.ds(pl.multiple_of(block * step, step), step)
        cross = jnp.dot(seen[...], anomaly_ref[:, span], preferred_element_type=f32)
        gain[:, span] = (cross * (weight_rows / count)).astype(bf16)

    @pl.loop(0, total_members // step)
    def _(block):
        span = pl.ds(pl.multiple_of(block * step, step), step)
        out_ref[span, :] = lax.dot_general(
            solved[:, span], gain[...], (((0,), (0,)), ((), ())), preferred_element_type=f32
        ).astype(bf16)


def whole(shape):
    return pl.BlockSpec(shape, lambda *_: (0,) * len(shape), memory_space=pltpu.VMEM)


def shards(
    prior_samples, measured_point, measured_reading, measurement_noise, noise_kind, taper_set
):
    members, bands, _, cells = prior_samples.shape
    tile = measured_point.shape[2]
    total = measurement_noise.shape[3]
    chunks = cells // LANES
    width = cells + LANES
    swap = [(0, 1), (1, 0)]

    own_noise = measurement_noise.reshape(tile, total)
    other_noise = lax.ppermute(own_noise, "region", swap)

    packed = pl.pallas_call(
        pack_members,
        grid=(bands // BANDS_PER_STEP,),
        in_specs=[
            pl.BlockSpec((members, BANDS_PER_STEP, chunks, LANES), lambda i: (0, i, 0, 0))
        ],
        out_specs=pl.BlockSpec((BANDS_PER_STEP, members, width), lambda i: (i, 0, 0)),
        out_shape=jax.ShapeDtypeStruct((bands, members, width), bf16),
        cost_estimate=pl.CostEstimate(
            flops=4 * members * bands * cells, bytes_accessed=7 * members * bands * cells, transcendentals=0
        ),
        compiler_params=pltpu.CompilerParams(vmem_limit_bytes=12 * MIB),
        name="pack_members",
    )(prior_samples.reshape(members, bands, chunks, LANES))

    packed, other_noise = lax.optimization_barrier((packed, other_noise))
    arrived = lax.all_to_all(packed, "member", split_axis=0, concat_axis=0, tiled=True)

    anomaly, seen = pl.pallas_call(
        observe,
        in_specs=[pl.BlockSpec(memory_space=pltpu.VMEM)] * 3,
        out_specs=[pl.BlockSpec(memory_space=pltpu.VMEM)] * 2,
        out_shape=[
            jax.ShapeDtypeStruct((total, cells), bf16),
            jax.ShapeDtypeStruct((tile, total + LANES), bf16),
        ],
        scratch_shapes=[
            pltpu.VMEM((bands, chunks, LANES), f32),
            pltpu.VMEM((bands, chunks, LANES), f32),
            pltpu.VMEM((tile, cells), bf16),
        ],
        compiler_params=pltpu.CompilerParams(vmem_limit_bytes=12 * MIB),
        name="observe",
    )(arrived, measured_point.reshape(1, tile), measured_reading.reshape(1, tile))

    other_seen = lax.ppermute(seen, "region", swap)

    increment = pl.pallas_call(
        analyse,
        in_specs=[pl.BlockSpec(memory_space=pltpu.SMEM)] * 2
        + [pl.BlockSpec(memory_space=pltpu.VMEM)] * 5,
        out_specs=pl.BlockSpec(memory_space=pltpu.VMEM),
        out_shape=jax.ShapeDtypeStruct((total, cells), bf16),
        scratch_shapes=[
            pltpu.VMEM((2 * tile, total), bf16),
            pltpu.VMEM((2 * tile, 2 * tile), bf16),
            pltpu.VMEM((2 * tile, cells), bf16),
            pltpu.VMEM((2 * tile, total), bf16),
            pltpu.VMEM((2 * tile, 256), f32),
            pltpu.VMEM((2 * tile, 256), f32),
            pltpu.VMEM((2 * tile, 256), f32),
        ],
        compiler_params=pltpu.CompilerParams(vmem_limit_bytes=20 * MIB),
        name="analyse",
    )(noise_kind, taper_set, anomaly, seen, other_seen, own_noise, other_noise)

    returned = lax.all_to_all(
        increment.reshape(bands, members, cells), "member", split_axis=0, concat_axis=0, tiled=True
    )

    unpacked = pl.pallas_call(
        unpack_members,
        grid=(bands // BANDS_PER_STEP,),
        in_specs=[pl.BlockSpec((BANDS_PER_STEP, members, cells), lambda i: (i, 0, 0))],
        out_specs=pl.BlockSpec((members, BANDS_PER_STEP, chunks, LANES), lambda i: (0, i, 0, 0)),
        out_shape=jax.ShapeDtypeStruct((members, bands, chunks, LANES), f32),
        compiler_params=pltpu.CompilerParams(vmem_limit_bytes=12 * MIB),
        name="unpack_members",
    )(returned)
    return unpacked.reshape(members, bands, 1, cells)


def solution(mesh):
    return jax.shard_map(
        shards,
        mesh=mesh,
        in_specs=(
            P("member", None, "region", None),
            P("member", "region", None),
            P("member", "region", None),
            P("member", "region", None, None),
            P("member", None),
            P("member", None),
        ),
        out_specs=P("member", None, "region", None),
        check_vma=False,
    )
```

```python
import jax
import jax.numpy as jnp
from jax import lax
from jax.experimental import pallas as pl
from jax.experimental.pallas import tpu as pltpu
from jax.sharding import PartitionSpec as P

ITERS = 4
TAPER_BASE = 0.7
LANES = 128
GROUPS = 8
COLUMNS = 512
MIB = 1024 * 1024

f32 = jnp.float32
bf16 = jnp.bfloat16


def split3(value):
    high = value.astype(bf16)
    rest = value - high.astype(f32)
    middle = rest.astype(bf16)
    low = (rest - middle.astype(f32)).astype(bf16)
    return high, middle, low


def row_order(rows, members, chunks):
    to = lax.broadcasted_iota(jnp.int32, (rows, rows), 0)
    source = lax.broadcasted_iota(jnp.int32, (rows, rows), 1)
    wanted = lax.rem(to, members) * chunks + lax.div(to, members)
    return jnp.where(source == wanted, 1.0, 0.0).astype(bf16)


def pack_members(x_ref, out_ref, held, arrived):
    members, bands, chunks, lanes = x_ref.shape
    cells = chunks * lanes
    rows = members * chunks
    groups = arrived.shape[0]
    per_group = bands // groups

    def fetch(group):
        span = pl.ds(group * per_group, per_group)
        return pltpu.make_async_copy(x_ref.at[:, span], held.at[:, span], arrived.at[group])

    for group in range(groups):
        fetch(group).start()
    order = row_order(rows, members, chunks)
    for group in range(groups):
        fetch(group).wait()
        for pair in range(group * per_group // 2, (group + 1) * per_group // 2):
            parts = []
            for band in (2 * pair, 2 * pair + 1):
                values = held[:, band]
                mean = jnp.sum(values, axis=0) * (1.0 / members)
                high = mean.astype(bf16)
                low = (mean - high.astype(f32)).astype(bf16)
                middle = high.astype(f32) + low.astype(f32)
                out_ref[band, :, cells : cells + lanes] = jnp.concatenate([high, low], axis=0)
                parts.append((values - middle[None]).reshape(rows, lanes).astype(bf16))
            moved = jnp.dot(
                order, jnp.concatenate(parts, axis=1), preferred_element_type=f32
            ).astype(bf16)
            for index in range(2):
                for chunk in range(chunks):
                    out_ref[2 * pair + index, :, chunk * lanes : (chunk + 1) * lanes] = moved[
                        chunk * members : (chunk + 1) * members,
                        index * lanes : (index + 1) * lanes,
                    ]


def unpack_members(x_ref, out_ref, held, sent):
    bands, members, cells = x_ref.shape
    chunks = cells // LANES
    rows = members * chunks
    groups = sent.shape[0]
    per_group = bands // groups
    order = row_order(rows, chunks, members)

    def put(group):
        span = pl.ds(group * per_group, per_group)
        return pltpu.make_async_copy(held.at[:, span], out_ref.at[:, span], sent.at[group])

    for group in range(groups):
        for pair in range(group * per_group // 2, (group + 1) * per_group // 2):
            parts = []
            for band in (2 * pair, 2 * pair + 1):
                parts.append(
                    jnp.concatenate(
                        [x_ref[band, :, c * LANES : (c + 1) * LANES] for c in range(chunks)], axis=0
                    )
                )
            moved = jnp.dot(order, jnp.concatenate(parts, axis=1), preferred_element_type=f32)
            for index in range(2):
                held[:, 2 * pair + index] = moved[
                    :, index * LANES : (index + 1) * LANES
                ].reshape(members, chunks, LANES)
        put(group).start()
    for group in range(groups):
        put(group).wait()


def observe(x_ref, points_ref, readings_ref, anomaly_ref, seen_ref, means, spread, hot):
    sources, members, width = x_ref.shape
    cells = anomaly_ref.shape[1]
    total_members = anomaly_ref.shape[0]
    chunks = cells // LANES
    obs = points_ref.shape[1]

    for source in range(sources):
        tail = x_ref[source, :, cells:width].astype(f32)
        means[source] = tail[:chunks] + tail[chunks:]
    average = jnp.sum(means[...], axis=0) * (1.0 / sources)

    points = jnp.transpose(jnp.broadcast_to(points_ref[...], (LANES, obs)))
    lane = lax.broadcasted_iota(jnp.int32, (obs, LANES), 1)
    picked = jnp.zeros((obs, LANES), f32)
    for chunk in range(chunks):
        here = points == lane + chunk * LANES
        hot[:, chunk * LANES : (chunk + 1) * LANES] = jnp.where(here, 1.0, 0.0).astype(bf16)
        picked = picked + jnp.where(here, average[chunk : chunk + 1, :], 0.0)
    readings = jnp.transpose(jnp.broadcast_to(readings_ref[...], (LANES, obs)))
    base = readings - jnp.sum(picked, axis=1, keepdims=True)
    high, middle, low = split3(base)
    seen_ref[:, total_members : total_members + LANES] = jnp.where(
        lane == 0, high.astype(f32), jnp.where(lane == 1, middle.astype(f32), low.astype(f32))
    ).astype(bf16)

    spread[...] = means[...] - average[None]

    per_block = 16

    @pl.loop(0, sources // per_block)
    def _(block):
        for inner in range(per_block):
            source = block * per_block + inner
            rows = pl.ds(pl.multiple_of(source * members, members), members)
            shift = spread[source]
            for chunk in range(chunks):
                columns = slice(chunk * LANES, (chunk + 1) * LANES)
                anomaly_ref[rows, columns] = (
                    x_ref[source, :, columns].astype(f32) + shift[chunk : chunk + 1, :]
                ).astype(bf16)
        size = per_block * members
        span = pl.ds(pl.multiple_of(block * size, size), size)
        seen_ref[:, span] = lax.dot_general(
            hot[...],
            anomaly_ref[span, :],
            (((1,), (1,)), ((), ())),
            preferred_element_type=f32,
        ).astype(bf16)


def analyse(
    kinds_ref,
    groups_ref,
    anomaly_ref,
    own_ref,
    other_ref,
    own_noise_ref,
    other_noise_ref,
    out_ref,
    seen,
    covariance,
    gain,
    solved,
    zero,
    one_step,
    two_steps,
):
    total_members, cells = anomaly_ref.shape
    tile = own_ref.shape[0]
    rows = 2 * tile
    region = lax.axis_index("region")
    own_kind = kinds_ref[0, region]
    other_kind = kinds_ref[0, 1 - region]
    one = jnp.int32(1)
    own_variance = 0.5 * lax.shift_left(one, own_kind).astype(f32)
    other_variance = 0.5 * lax.shift_left(one, other_kind).astype(f32)
    cross_weight = jnp.where(groups_ref[0, 0] == groups_ref[0, 1], f32(TAPER_BASE), f32(0.0))
    count = total_members - 1

    seen[:tile, :] = own_ref[:, :total_members]
    seen[tile:, :] = other_ref[:, :total_members]
    in_own = lax.broadcasted_iota(jnp.int32, (rows, 1), 0) < tile
    variance = jnp.where(in_own, own_variance, other_variance)
    weight_rows = jnp.where(in_own, f32(1.0), cross_weight)

    product = lax.dot_general(
        seen[...], seen[...], (((1,), (1,)), ((), ())), preferred_element_type=f32
    )
    for half in range(2):
        columns = slice(half * tile, (half + 1) * tile)
        weight = jnp.where(in_own == (half == 0), f32(1.0), cross_weight)
        covariance[:, columns] = (product[:, columns] * (weight / count)).astype(bf16)
    bound = variance + jnp.sum(jnp.abs(covariance[...].astype(f32)), axis=1, keepdims=True)
    largest = jnp.max(bound)
    lowest = jnp.minimum(own_variance, other_variance)
    highest = lowest + largest
    center = 0.5 * (highest + lowest)
    radius = 0.5 * (highest - lowest)
    sigma = center / radius
    rho = 1.0 / sigma

    own_base = jnp.sum(own_ref[:, total_members:].astype(f32)[:, :3], axis=1, keepdims=True)
    other_base = jnp.sum(other_ref[:, total_members:].astype(f32)[:, :3], axis=1, keepdims=True)
    own_scale = jnp.sqrt(jnp.full((1, 1), own_variance, f32))
    other_scale = jnp.sqrt(jnp.full((1, 1), other_variance, f32))
    width = COLUMNS

    steps = []
    reach_before, keep_before = 1.0 / center, f32(0.0)
    for _ in range(ITERS - 1):
        rho_next = 1.0 / (2.0 * sigma - rho)
        keep = rho_next * rho
        reach = 2.0 * rho_next / radius
        ratio = reach / reach_before
        steps.append((keep + ratio - reach * variance, ratio * keep_before, reach))
        rho, reach_before, keep_before = rho_next, reach, keep
    inverse = 1.0 / center

    spans = [slice(start, start + width) for start in range(0, total_members, width)]
    for span in spans:
        zero[:tile, span] = inverse * (
            own_base + own_scale * own_noise_ref[:, span].astype(f32) - own_ref[:, span].astype(f32)
        )
        zero[tile:, span] = inverse * (
            other_base
            + other_scale * other_noise_ref[:, span].astype(f32)
            - other_ref[:, span].astype(f32)
        )

    def apply(held, span):
        return jnp.dot(
            covariance[...], held[:, span].astype(bf16), preferred_element_type=f32
        )

    for span in spans:
        ahead, _, reach = steps[0]
        one_step[:, span] = ahead * zero[:, span] - reach * apply(zero, span)
    for span in spans:
        ahead, back, reach = steps[1]
        two_steps[:, span] = (
            ahead * one_step[:, span] - back * zero[:, span] - reach * apply(one_step, span)
        )
    for span in spans:
        ahead, back, reach = steps[2]
        solved[:, span] = (
            (1.0 + ahead) * two_steps[:, span]
            + (1.0 - back) * one_step[:, span]
            + zero[:, span]
            - reach * apply(two_steps, span)
        ).astype(bf16)

    cross = jnp.dot(seen[...], anomaly_ref[...], preferred_element_type=f32)
    gain[...] = (cross * (weight_rows / count)).astype(bf16)
    out_ref[...] = lax.dot_general(
        solved[...], gain[...], (((0,), (0,)), ((), ())), preferred_element_type=f32
    ).astype(bf16)


def shards(
    prior_samples, measured_point, measured_reading, measurement_noise, noise_kind, taper_set
):
    members, bands, _, cells = prior_samples.shape
    tile = measured_point.shape[2]
    total = measurement_noise.shape[3]
    chunks = cells // LANES
    width = cells + LANES
    swap = [(0, 1), (1, 0)]

    own_noise = measurement_noise.reshape(tile, total)
    other_noise = lax.ppermute(own_noise, "region", swap)

    packed = pl.pallas_call(
        pack_members,
        in_specs=[pl.BlockSpec(memory_space=pltpu.HBM)],
        out_specs=pl.BlockSpec(memory_space=pltpu.VMEM),
        out_shape=jax.ShapeDtypeStruct((bands, members, width), bf16),
        scratch_shapes=[
            pltpu.VMEM((members, bands, chunks, LANES), f32),
            pltpu.SemaphoreType.DMA((GROUPS,)),
        ],
        cost_estimate=pl.CostEstimate(
            flops=4 * members * bands * cells, bytes_accessed=7 * members * bands * cells, transcendentals=0
        ),
        compiler_params=pltpu.CompilerParams(vmem_limit_bytes=57 * MIB),
        name="pack_members",
    )(prior_samples.reshape(members, bands, chunks, LANES))

    packed, other_noise = lax.optimization_barrier((packed, other_noise))
    arrived = lax.all_to_all(packed, "member", split_axis=0, concat_axis=0, tiled=True)

    anomaly, seen = pl.pallas_call(
        observe,
        in_specs=[pl.BlockSpec(memory_space=pltpu.VMEM)] * 3,
        out_specs=[pl.BlockSpec(memory_space=pltpu.VMEM)] * 2,
        out_shape=[
            jax.ShapeDtypeStruct((total, cells), bf16),
            jax.ShapeDtypeStruct((tile, total + LANES), bf16),
        ],
        scratch_shapes=[
            pltpu.VMEM((bands, chunks, LANES), f32),
            pltpu.VMEM((bands, chunks, LANES), f32),
            pltpu.VMEM((tile, cells), bf16),
        ],
        compiler_params=pltpu.CompilerParams(vmem_limit_bytes=12 * MIB),
        name="observe",
    )(arrived, measured_point.reshape(1, tile), measured_reading.reshape(1, tile))

    other_seen = lax.ppermute(seen, "region", swap)

    increment = pl.pallas_call(
        analyse,
        in_specs=[pl.BlockSpec(memory_space=pltpu.SMEM)] * 2
        + [pl.BlockSpec(memory_space=pltpu.VMEM)] * 5,
        out_specs=pl.BlockSpec(memory_space=pltpu.VMEM),
        out_shape=jax.ShapeDtypeStruct((total, cells), bf16),
        scratch_shapes=[
            pltpu.VMEM((2 * tile, total), bf16),
            pltpu.VMEM((2 * tile, 2 * tile), bf16),
            pltpu.VMEM((2 * tile, cells), bf16),
            pltpu.VMEM((2 * tile, total), bf16),
            pltpu.VMEM((2 * tile, total), f32),
            pltpu.VMEM((2 * tile, total), f32),
            pltpu.VMEM((2 * tile, total), f32),
        ],
        compiler_params=pltpu.CompilerParams(vmem_limit_bytes=28 * MIB),
        name="analyse",
    )(noise_kind, taper_set, anomaly, seen, other_seen, own_noise, other_noise)

    returned = lax.all_to_all(
        increment.reshape(bands, members, cells), "member", split_axis=0, concat_axis=0, tiled=True
    )

    unpacked = pl.pallas_call(
        unpack_members,
        in_specs=[pl.BlockSpec(memory_space=pltpu.VMEM)],
        out_specs=pl.BlockSpec(memory_space=pltpu.HBM),
        out_shape=jax.ShapeDtypeStruct((members, bands, chunks, LANES), f32),
        scratch_shapes=[
            pltpu.VMEM((members, bands, chunks, LANES), f32),
            pltpu.SemaphoreType.DMA((GROUPS,)),
        ],
        compiler_params=pltpu.CompilerParams(vmem_limit_bytes=12 * MIB),
        name="unpack_members",
    )(returned)
    return unpacked.reshape(members, bands, 1, cells)


def solution(mesh):
    return jax.shard_map(
        shards,
        mesh=mesh,
        in_specs=(
            P("member", None, "region", None),
            P("member", "region", None),
            P("member", "region", None),
            P("member", "region", None, None),
            P("member", None),
            P("member", None),
        ),
        out_specs=P("member", None, "region", None),
        check_vma=False,
    )
```

```python
import jax
import jax.numpy as jnp
from jax import lax
from jax.experimental import pallas as pl
from jax.experimental.pallas import tpu as pltpu
from jax.sharding import PartitionSpec as P

ITERS = 4
TAPER_BASE = 0.7
LANES = 128
GROUPS = 8
COLUMNS = 512
MIB = 1024 * 1024

STRIDE = 13

f32 = jnp.float32
bf16 = jnp.bfloat16


def group_order(devices):
    return [STRIDE * place % devices for place in range(devices)]


def place_of(devices):
    places = [0] * devices
    for place, device in enumerate(group_order(devices)):
        places[device] = place
    return places


def exchange(value):
    order = group_order(value.shape[0])
    return lax.all_to_all(
        value, "member", split_axis=0, concat_axis=0, axis_index_groups=[order], tiled=True
    )


def split3(value):
    high = value.astype(bf16)
    rest = value - high.astype(f32)
    middle = rest.astype(bf16)
    low = (rest - middle.astype(f32)).astype(bf16)
    return high, middle, low


def row_order(rows, members, chunks):
    to = lax.broadcasted_iota(jnp.int32, (rows, rows), 0)
    source = lax.broadcasted_iota(jnp.int32, (rows, rows), 1)
    wanted = lax.rem(to, members) * chunks + lax.div(to, members)
    return jnp.where(source == wanted, 1.0, 0.0).astype(bf16)


def pack_members(x_ref, out_ref, held, arrived):
    members, bands, chunks, lanes = x_ref.shape
    cells = chunks * lanes
    rows = members * chunks
    groups = arrived.shape[0]
    per_group = bands // groups

    def fetch(group):
        span = pl.ds(group * per_group, per_group)
        return pltpu.make_async_copy(x_ref.at[:, span], held.at[:, span], arrived.at[group])

    for group in range(groups):
        fetch(group).start()
    order = row_order(rows, members, chunks)
    place = place_of(bands)
    for group in range(groups):
        fetch(group).wait()
        for pair in range(group * per_group // 2, (group + 1) * per_group // 2):
            parts = []
            for band in (2 * pair, 2 * pair + 1):
                values = held[:, band]
                mean = jnp.sum(values, axis=0) * (1.0 / members)
                high = mean.astype(bf16)
                low = (mean - high.astype(f32)).astype(bf16)
                middle = high.astype(f32) + low.astype(f32)
                out_ref[place[band], :, cells : cells + lanes] = jnp.concatenate([high, low], axis=0)
                parts.append((values - middle[None]).reshape(rows, lanes).astype(bf16))
            moved = jnp.dot(
                order, jnp.concatenate(parts, axis=1), preferred_element_type=f32
            ).astype(bf16)
            for index in range(2):
                for chunk in range(chunks):
                    out_ref[place[2 * pair + index], :, chunk * lanes : (chunk + 1) * lanes] = moved[
                        chunk * members : (chunk + 1) * members,
                        index * lanes : (index + 1) * lanes,
                    ]


def unpack_members(x_ref, out_ref, held, sent):
    bands, members, cells = x_ref.shape
    chunks = cells // LANES
    rows = members * chunks
    groups = sent.shape[0]
    per_group = bands // groups
    order = row_order(rows, chunks, members)
    place = place_of(bands)

    def put(group):
        span = pl.ds(group * per_group, per_group)
        return pltpu.make_async_copy(held.at[:, span], out_ref.at[:, span], sent.at[group])

    for group in range(groups):
        for pair in range(group * per_group // 2, (group + 1) * per_group // 2):
            parts = []
            for band in (2 * pair, 2 * pair + 1):
                parts.append(
                    jnp.concatenate(
                        [
                            x_ref[place[band], :, c * LANES : (c + 1) * LANES]
                            for c in range(chunks)
                        ], axis=0
                    )
                )
            moved = jnp.dot(order, jnp.concatenate(parts, axis=1), preferred_element_type=f32)
            for index in range(2):
                held[:, 2 * pair + index] = moved[
                    :, index * LANES : (index + 1) * LANES
                ].reshape(members, chunks, LANES)
        put(group).start()
    for group in range(groups):
        put(group).wait()


def observe(x_ref, points_ref, readings_ref, anomaly_ref, seen_ref, means, spread, hot):
    sources, members, width = x_ref.shape
    cells = anomaly_ref.shape[1]
    total_members = anomaly_ref.shape[0]
    chunks = cells // LANES
    obs = points_ref.shape[1]

    place = place_of(sources)
    for source in range(sources):
        tail = x_ref[place[source], :, cells:width].astype(f32)
        means[source] = tail[:chunks] + tail[chunks:]
    average = jnp.sum(means[...], axis=0) * (1.0 / sources)

    points = jnp.transpose(jnp.broadcast_to(points_ref[...], (LANES, obs)))
    lane = lax.broadcasted_iota(jnp.int32, (obs, LANES), 1)
    picked = jnp.zeros((obs, LANES), f32)
    for chunk in range(chunks):
        here = points == lane + chunk * LANES
        hot[:, chunk * LANES : (chunk + 1) * LANES] = jnp.where(here, 1.0, 0.0).astype(bf16)
        picked = picked + jnp.where(here, average[chunk : chunk + 1, :], 0.0)
    readings = jnp.transpose(jnp.broadcast_to(readings_ref[...], (LANES, obs)))
    base = readings - jnp.sum(picked, axis=1, keepdims=True)
    high, middle, low = split3(base)
    seen_ref[:, total_members : total_members + LANES] = jnp.where(
        lane == 0, high.astype(f32), jnp.where(lane == 1, middle.astype(f32), low.astype(f32))
    ).astype(bf16)

    spread[...] = means[...] - average[None]

    for source in range(sources):
        rows = slice(source * members, (source + 1) * members)
        shift = spread[source]
        for chunk in range(chunks):
            columns = slice(chunk * LANES, (chunk + 1) * LANES)
            anomaly_ref[rows, columns] = (
                x_ref[place[source], :, columns].astype(f32) + shift[chunk : chunk + 1, :]
            ).astype(bf16)
    for start in range(0, total_members, COLUMNS):
        span = slice(start, start + COLUMNS)
        seen_ref[:, span] = lax.dot_general(
            hot[...],
            anomaly_ref[span, :],
            (((1,), (1,)), ((), ())),
            preferred_element_type=f32,
        ).astype(bf16)


def analyse(
    kinds_ref,
    groups_ref,
    anomaly_ref,
    own_ref,
    other_ref,
    own_noise_ref,
    other_noise_ref,
    out_ref,
    seen,
    covariance,
    gain,
    solved,
    zero,
    one_step,
    two_steps,
):
    total_members, cells = anomaly_ref.shape
    tile = own_ref.shape[0]
    rows = 2 * tile
    region = lax.axis_index("region")
    own_kind = kinds_ref[0, region]
    other_kind = kinds_ref[0, 1 - region]
    one = jnp.int32(1)
    own_variance = 0.5 * lax.shift_left(one, own_kind).astype(f32)
    other_variance = 0.5 * lax.shift_left(one, other_kind).astype(f32)
    cross_weight = jnp.where(groups_ref[0, 0] == groups_ref[0, 1], f32(TAPER_BASE), f32(0.0))
    count = total_members - 1

    seen[:tile, :] = own_ref[:, :total_members]
    seen[tile:, :] = other_ref[:, :total_members]
    in_own = lax.broadcasted_iota(jnp.int32, (rows, 1), 0) < tile
    variance = jnp.where(in_own, own_variance, other_variance)
    weight_rows = jnp.where(in_own, f32(1.0), cross_weight)

    product = lax.dot_general(
        seen[...], seen[...], (((1,), (1,)), ((), ())), preferred_element_type=f32
    )
    for half in range(2):
        columns = slice(half * tile, (half + 1) * tile)
        weight = jnp.where(in_own == (half == 0), f32(1.0), cross_weight)
        covariance[:, columns] = (product[:, columns] * (weight / count)).astype(bf16)
    bound = variance + jnp.sum(jnp.abs(covariance[...].astype(f32)), axis=1, keepdims=True)
    largest = jnp.max(bound)
    lowest = jnp.minimum(own_variance, other_variance)
    highest = lowest + largest
    center = 0.5 * (highest + lowest)
    radius = 0.5 * (highest - lowest)
    sigma = center / radius
    rho = 1.0 / sigma

    own_base = jnp.sum(own_ref[:, total_members:].astype(f32)[:, :3], axis=1, keepdims=True)
    other_base = jnp.sum(other_ref[:, total_members:].astype(f32)[:, :3], axis=1, keepdims=True)
    own_scale = jnp.sqrt(jnp.full((1, 1), own_variance, f32))
    other_scale = jnp.sqrt(jnp.full((1, 1), other_variance, f32))
    width = COLUMNS

    steps = []
    reach_before, keep_before = 1.0 / center, f32(0.0)
    for _ in range(ITERS - 1):
        rho_next = 1.0 / (2.0 * sigma - rho)
        keep = rho_next * rho
        reach = 2.0 * rho_next / radius
        ratio = reach / reach_before
        steps.append((keep + ratio - reach * variance, ratio * keep_before, reach))
        rho, reach_before, keep_before = rho_next, reach, keep
    inverse = 1.0 / center

    spans = [slice(start, start + width) for start in range(0, total_members, width)]
    for span in spans:
        zero[:tile, span] = inverse * (
            own_base + own_scale * own_noise_ref[:, span].astype(f32) - own_ref[:, span].astype(f32)
        )
        zero[tile:, span] = inverse * (
            other_base
            + other_scale * other_noise_ref[:, span].astype(f32)
            - other_ref[:, span].astype(f32)
        )

    def apply(held, span):
        return jnp.dot(
            covariance[...], held[:, span].astype(bf16), preferred_element_type=f32
        )

    for span in spans:
        ahead, _, reach = steps[0]
        one_step[:, span] = ahead * zero[:, span] - reach * apply(zero, span)
    for span in spans:
        ahead, back, reach = steps[1]
        two_steps[:, span] = (
            ahead * one_step[:, span] - back * zero[:, span] - reach * apply(one_step, span)
        )
    for span in spans:
        ahead, back, reach = steps[2]
        solved[:, span] = (
            (1.0 + ahead) * two_steps[:, span]
            + (1.0 - back) * one_step[:, span]
            + zero[:, span]
            - reach * apply(two_steps, span)
        ).astype(bf16)

    cross = jnp.dot(seen[...], anomaly_ref[...], preferred_element_type=f32)
    gain[...] = (cross * (weight_rows / count)).astype(bf16)
    increment = lax.dot_general(
        solved[...], gain[...], (((0,), (0,)), ((), ())), preferred_element_type=f32
    ).astype(bf16)
    devices, members, _ = out_ref.shape
    for device, place in enumerate(place_of(devices)):
        out_ref[place] = increment[device * members : (device + 1) * members]


def shards(
    prior_samples, measured_point, measured_reading, measurement_noise, noise_kind, taper_set
):
    members, bands, _, cells = prior_samples.shape
    tile = measured_point.shape[2]
    total = measurement_noise.shape[3]
    chunks = cells // LANES
    width = cells + LANES
    swap = [(0, 1), (1, 0)]

    own_noise = measurement_noise.reshape(tile, total)
    other_noise = lax.ppermute(own_noise, "region", swap)

    packed = pl.pallas_call(
        pack_members,
        in_specs=[pl.BlockSpec(memory_space=pltpu.HBM)],
        out_specs=pl.BlockSpec(memory_space=pltpu.VMEM),
        out_shape=jax.ShapeDtypeStruct((bands, members, width), bf16),
        scratch_shapes=[
            pltpu.VMEM((members, bands, chunks, LANES), f32),
            pltpu.SemaphoreType.DMA((GROUPS,)),
        ],
        cost_estimate=pl.CostEstimate(
            flops=4 * members * bands * cells, bytes_accessed=7 * members * bands * cells, transcendentals=0
        ),
        compiler_params=pltpu.CompilerParams(vmem_limit_bytes=50 * MIB),
        name="pack_members",
    )(prior_samples.reshape(members, bands, chunks, LANES))

    packed, other_noise = lax.optimization_barrier((packed, other_noise))
    arrived = exchange(packed)

    anomaly, seen = pl.pallas_call(
        observe,
        in_specs=[pl.BlockSpec(memory_space=pltpu.VMEM)] * 3,
        out_specs=[pl.BlockSpec(memory_space=pltpu.VMEM)] * 2,
        out_shape=[
            jax.ShapeDtypeStruct((total, cells), bf16),
            jax.ShapeDtypeStruct((tile, total + LANES), bf16),
        ],
        scratch_shapes=[
            pltpu.VMEM((bands, chunks, LANES), f32),
            pltpu.VMEM((bands, chunks, LANES), f32),
            pltpu.VMEM((tile, cells), bf16),
        ],
        compiler_params=pltpu.CompilerParams(vmem_limit_bytes=12 * MIB),
        name="observe",
    )(arrived, measured_point.reshape(1, tile), measured_reading.reshape(1, tile))

    other_seen = lax.ppermute(seen, "region", swap)

    increment = pl.pallas_call(
        analyse,
        in_specs=[pl.BlockSpec(memory_space=pltpu.SMEM)] * 2
        + [pl.BlockSpec(memory_space=pltpu.VMEM)] * 5,
        out_specs=pl.BlockSpec(memory_space=pltpu.VMEM),
        out_shape=jax.ShapeDtypeStruct((bands, members, cells), bf16),
        scratch_shapes=[
            pltpu.VMEM((2 * tile, total), bf16),
            pltpu.VMEM((2 * tile, 2 * tile), bf16),
            pltpu.VMEM((2 * tile, cells), bf16),
            pltpu.VMEM((2 * tile, total), bf16),
            pltpu.VMEM((2 * tile, total), f32),
            pltpu.VMEM((2 * tile, total), f32),
            pltpu.VMEM((2 * tile, total), f32),
        ],
        compiler_params=pltpu.CompilerParams(vmem_limit_bytes=28 * MIB),
        name="analyse",
    )(noise_kind, taper_set, anomaly, seen, other_seen, own_noise, other_noise)

    returned = exchange(increment)

    unpacked = pl.pallas_call(
        unpack_members,
        in_specs=[pl.BlockSpec(memory_space=pltpu.VMEM)],
        out_specs=pl.BlockSpec(memory_space=pltpu.HBM),
        out_shape=jax.ShapeDtypeStruct((members, bands, chunks, LANES), f32),
        scratch_shapes=[
            pltpu.VMEM((members, bands, chunks, LANES), f32),
            pltpu.SemaphoreType.DMA((GROUPS,)),
        ],
        compiler_params=pltpu.CompilerParams(vmem_limit_bytes=12 * MIB),
        name="unpack_members",
    )(returned)
    return unpacked.reshape(members, bands, 1, cells)


def solution(mesh):
    return jax.shard_map(
        shards,
        mesh=mesh,
        in_specs=(
            P("member", None, "region", None),
            P("member", "region", None),
            P("member", "region", None),
            P("member", "region", None, None),
            P("member", None),
            P("member", None),
        ),
        out_specs=P("member", None, "region", None),
        check_vma=False,
    )
```

```python
import jax
import jax.numpy as jnp
from jax import lax
from jax.experimental import pallas as pl
from jax.experimental.pallas import tpu as pltpu
from jax.sharding import PartitionSpec as P

ITERS = 4
TAPER_BASE = 0.7
LANES = 128
GROUPS = 8
COLUMNS = 512
MIB = 1024 * 1024

STRIDE = 21

f32 = jnp.float32
bf16 = jnp.bfloat16


def group_order(devices):
    return [STRIDE * place % devices for place in range(devices)]


def place_of(devices):
    places = [0] * devices
    for place, device in enumerate(group_order(devices)):
        places[device] = place
    return places


def exchange(value):
    order = group_order(value.shape[0])
    return lax.all_to_all(
        value, "member", split_axis=0, concat_axis=0, axis_index_groups=[order], tiled=True
    )


def split3(value):
    high = value.astype(bf16)
    rest = value - high.astype(f32)
    middle = rest.astype(bf16)
    low = (rest - middle.astype(f32)).astype(bf16)
    return high, middle, low


def row_order(rows, members, chunks):
    to = lax.broadcasted_iota(jnp.int32, (rows, rows), 0)
    source = lax.broadcasted_iota(jnp.int32, (rows, rows), 1)
    wanted = lax.rem(to, members) * chunks + lax.div(to, members)
    return jnp.where(source == wanted, 1.0, 0.0).astype(bf16)


def pack_members(x_ref, out_ref, held, arrived):
    members, bands, chunks, lanes = x_ref.shape
    cells = chunks * lanes
    rows = members * chunks
    groups = arrived.shape[0]
    per_group = bands // groups

    def fetch(group):
        span = pl.ds(group * per_group, per_group)
        return pltpu.make_async_copy(x_ref.at[:, span], held.at[:, span], arrived.at[group])

    for group in range(groups):
        fetch(group).start()
    order = row_order(rows, members, chunks)
    place = place_of(bands)
    for group in range(groups):
        fetch(group).wait()
        for pair in range(group * per_group // 2, (group + 1) * per_group // 2):
            parts = []
            for band in (2 * pair, 2 * pair + 1):
                values = held[:, band]
                mean = jnp.sum(values, axis=0) * (1.0 / members)
                high = mean.astype(bf16)
                low = (mean - high.astype(f32)).astype(bf16)
                middle = high.astype(f32) + low.astype(f32)
                out_ref[place[band], :, cells : cells + lanes] = jnp.concatenate([high, low], axis=0)
                parts.append((values - middle[None]).reshape(rows, lanes).astype(bf16))
            moved = jnp.dot(
                order, jnp.concatenate(parts, axis=1), preferred_element_type=f32
            ).astype(bf16)
            for index in range(2):
                for chunk in range(chunks):
                    out_ref[place[2 * pair + index], :, chunk * lanes : (chunk + 1) * lanes] = moved[
                        chunk * members : (chunk + 1) * members,
                        index * lanes : (index + 1) * lanes,
                    ]


def unpack_members(x_ref, out_ref, held, sent):
    bands, members, cells = x_ref.shape
    chunks = cells // LANES
    rows = members * chunks
    groups = sent.shape[0]
    per_group = bands // groups
    order = row_order(rows, chunks, members)
    place = place_of(bands)

    def put(group):
        span = pl.ds(group * per_group, per_group)
        return pltpu.make_async_copy(held.at[:, span], out_ref.at[:, span], sent.at[group])

    for group in range(groups):
        for pair in range(group * per_group // 2, (group + 1) * per_group // 2):
            parts = []
            for band in (2 * pair, 2 * pair + 1):
                parts.append(
                    jnp.concatenate(
                        [
                            x_ref[place[band], :, c * LANES : (c + 1) * LANES]
                            for c in range(chunks)
                        ], axis=0
                    )
                )
            moved = jnp.dot(order, jnp.concatenate(parts, axis=1), preferred_element_type=f32)
            for index in range(2):
                held[:, 2 * pair + index] = moved[
                    :, index * LANES : (index + 1) * LANES
                ].reshape(members, chunks, LANES)
        put(group).start()
    for group in range(groups):
        put(group).wait()


def observe(x_ref, points_ref, readings_ref, anomaly_ref, seen_ref, means, spread, hot):
    sources, members, width = x_ref.shape
    cells = anomaly_ref.shape[1]
    total_members = anomaly_ref.shape[0]
    chunks = cells // LANES
    obs = points_ref.shape[1]

    place = place_of(sources)
    for source in range(sources):
        tail = x_ref[place[source], :, cells:width].astype(f32)
        means[source] = tail[:chunks] + tail[chunks:]
    average = jnp.sum(means[...], axis=0) * (1.0 / sources)

    points = jnp.transpose(jnp.broadcast_to(points_ref[...], (LANES, obs)))
    lane = lax.broadcasted_iota(jnp.int32, (obs, LANES), 1)
    picked = jnp.zeros((obs, LANES), f32)
    for chunk in range(chunks):
        here = points == lane + chunk * LANES
        hot[:, chunk * LANES : (chunk + 1) * LANES] = jnp.where(here, 1.0, 0.0).astype(bf16)
        picked = picked + jnp.where(here, average[chunk : chunk + 1, :], 0.0)
    readings = jnp.transpose(jnp.broadcast_to(readings_ref[...], (LANES, obs)))
    base = readings - jnp.sum(picked, axis=1, keepdims=True)
    high, middle, low = split3(base)
    seen_ref[:, total_members : total_members + LANES] = jnp.where(
        lane == 0, high.astype(f32), jnp.where(lane == 1, middle.astype(f32), low.astype(f32))
    ).astype(bf16)

    spread[...] = means[...] - average[None]

    for source in range(sources):
        rows = slice(source * members, (source + 1) * members)
        shift = spread[source]
        for chunk in range(chunks):
            columns = slice(chunk * LANES, (chunk + 1) * LANES)
            anomaly_ref[rows, columns] = (
                x_ref[place[source], :, columns].astype(f32) + shift[chunk : chunk + 1, :]
            ).astype(bf16)
    for start in range(0, total_members, COLUMNS):
        span = slice(start, start + COLUMNS)
        seen_ref[:, span] = lax.dot_general(
            hot[...],
            anomaly_ref[span, :],
            (((1,), (1,)), ((), ())),
            preferred_element_type=f32,
        ).astype(bf16)


def analyse(
    kinds_ref,
    groups_ref,
    anomaly_ref,
    own_ref,
    other_ref,
    own_noise_ref,
    other_noise_ref,
    out_ref,
    seen,
    covariance,
    gain,
    solved,
    zero,
    one_step,
    two_steps,
):
    total_members, cells = anomaly_ref.shape
    tile = own_ref.shape[0]
    rows = 2 * tile
    region = lax.axis_index("region")
    own_kind = kinds_ref[0, region]
    other_kind = kinds_ref[0, 1 - region]
    one = jnp.int32(1)
    own_variance = 0.5 * lax.shift_left(one, own_kind).astype(f32)
    other_variance = 0.5 * lax.shift_left(one, other_kind).astype(f32)
    cross_weight = jnp.where(groups_ref[0, 0] == groups_ref[0, 1], f32(TAPER_BASE), f32(0.0))
    count = total_members - 1

    seen[:tile, :] = own_ref[:, :total_members]
    seen[tile:, :] = other_ref[:, :total_members]
    in_own = lax.broadcasted_iota(jnp.int32, (rows, 1), 0) < tile
    variance = jnp.where(in_own, own_variance, other_variance)
    weight_rows = jnp.where(in_own, f32(1.0), cross_weight)

    product = lax.dot_general(
        seen[...], seen[...], (((1,), (1,)), ((), ())), preferred_element_type=f32
    )
    for half in range(2):
        columns = slice(half * tile, (half + 1) * tile)
        weight = jnp.where(in_own == (half == 0), f32(1.0), cross_weight)
        covariance[:, columns] = (product[:, columns] * (weight / count)).astype(bf16)
    bound = variance + jnp.sum(jnp.abs(covariance[...].astype(f32)), axis=1, keepdims=True)
    largest = jnp.max(bound)
    lowest = jnp.minimum(own_variance, other_variance)
    highest = lowest + largest
    center = 0.5 * (highest + lowest)
    radius = 0.5 * (highest - lowest)
    sigma = center / radius
    rho = 1.0 / sigma

    own_base = jnp.sum(own_ref[:, total_members:].astype(f32)[:, :3], axis=1, keepdims=True)
    other_base = jnp.sum(other_ref[:, total_members:].astype(f32)[:, :3], axis=1, keepdims=True)
    own_scale = jnp.sqrt(jnp.full((1, 1), own_variance, f32))
    other_scale = jnp.sqrt(jnp.full((1, 1), other_variance, f32))
    width = COLUMNS

    steps = []
    reach_before, keep_before = 1.0 / center, f32(0.0)
    for _ in range(ITERS - 1):
        rho_next = 1.0 / (2.0 * sigma - rho)
        keep = rho_next * rho
        reach = 2.0 * rho_next / radius
        ratio = reach / reach_before
        steps.append((keep + ratio - reach * variance, ratio * keep_before, reach))
        rho, reach_before, keep_before = rho_next, reach, keep
    inverse = 1.0 / center

    spans = [slice(start, start + width) for start in range(0, total_members, width)]
    for span in spans:
        zero[:tile, span] = inverse * (
            own_base + own_scale * own_noise_ref[:, span].astype(f32) - own_ref[:, span].astype(f32)
        )
        zero[tile:, span] = inverse * (
            other_base
            + other_scale * other_noise_ref[:, span].astype(f32)
            - other_ref[:, span].astype(f32)
        )

    def apply(held, span):
        return jnp.dot(
            covariance[...], held[:, span].astype(bf16), preferred_element_type=f32
        )

    for span in spans:
        ahead, _, reach = steps[0]
        one_step[:, span] = ahead * zero[:, span] - reach * apply(zero, span)
    for span in spans:
        ahead, back, reach = steps[1]
        two_steps[:, span] = (
            ahead * one_step[:, span] - back * zero[:, span] - reach * apply(one_step, span)
        )
    for span in spans:
        ahead, back, reach = steps[2]
        solved[:, span] = (
            (1.0 + ahead) * two_steps[:, span]
            + (1.0 - back) * one_step[:, span]
            + zero[:, span]
            - reach * apply(two_steps, span)
        ).astype(bf16)

    cross = jnp.dot(seen[...], anomaly_ref[...], preferred_element_type=f32)
    gain[...] = (cross * (weight_rows / count)).astype(bf16)
    increment = lax.dot_general(
        solved[...], gain[...], (((0,), (0,)), ((), ())), preferred_element_type=f32
    ).astype(bf16)
    devices, members, _ = out_ref.shape
    for device, place in enumerate(place_of(devices)):
        out_ref[place] = increment[device * members : (device + 1) * members]


def shards(
    prior_samples, measured_point, measured_reading, measurement_noise, noise_kind, taper_set
):
    members, bands, _, cells = prior_samples.shape
    tile = measured_point.shape[2]
    total = measurement_noise.shape[3]
    chunks = cells // LANES
    width = cells + LANES
    swap = [(0, 1), (1, 0)]

    own_noise = measurement_noise.reshape(tile, total)
    other_noise = lax.ppermute(own_noise, "region", swap)

    packed = pl.pallas_call(
        pack_members,
        in_specs=[pl.BlockSpec(memory_space=pltpu.HBM)],
        out_specs=pl.BlockSpec(memory_space=pltpu.VMEM),
        out_shape=jax.ShapeDtypeStruct((bands, members, width), bf16),
        scratch_shapes=[
            pltpu.VMEM((members, bands, chunks, LANES), f32),
            pltpu.SemaphoreType.DMA((GROUPS,)),
        ],
        cost_estimate=pl.CostEstimate(
            flops=4 * members * bands * cells, bytes_accessed=7 * members * bands * cells, transcendentals=0
        ),
        compiler_params=pltpu.CompilerParams(vmem_limit_bytes=50 * MIB),
        name="pack_members",
    )(prior_samples.reshape(members, bands, chunks, LANES))

    packed, other_noise = lax.optimization_barrier((packed, other_noise))
    arrived = exchange(packed)

    anomaly, seen = pl.pallas_call(
        observe,
        in_specs=[pl.BlockSpec(memory_space=pltpu.VMEM)] * 3,
        out_specs=[pl.BlockSpec(memory_space=pltpu.VMEM)] * 2,
        out_shape=[
            jax.ShapeDtypeStruct((total, cells), bf16),
            jax.ShapeDtypeStruct((tile, total + LANES), bf16),
        ],
        scratch_shapes=[
            pltpu.VMEM((bands, chunks, LANES), f32),
            pltpu.VMEM((bands, chunks, LANES), f32),
            pltpu.VMEM((tile, cells), bf16),
        ],
        compiler_params=pltpu.CompilerParams(vmem_limit_bytes=12 * MIB),
        name="observe",
    )(arrived, measured_point.reshape(1, tile), measured_reading.reshape(1, tile))

    other_seen = lax.ppermute(seen, "region", swap)

    increment = pl.pallas_call(
        analyse,
        in_specs=[pl.BlockSpec(memory_space=pltpu.SMEM)] * 2
        + [pl.BlockSpec(memory_space=pltpu.VMEM)] * 5,
        out_specs=pl.BlockSpec(memory_space=pltpu.VMEM),
        out_shape=jax.ShapeDtypeStruct((bands, members, cells), bf16),
        scratch_shapes=[
            pltpu.VMEM((2 * tile, total), bf16),
            pltpu.VMEM((2 * tile, 2 * tile), bf16),
            pltpu.VMEM((2 * tile, cells), bf16),
            pltpu.VMEM((2 * tile, total), bf16),
            pltpu.VMEM((2 * tile, total), f32),
            pltpu.VMEM((2 * tile, total), f32),
            pltpu.VMEM((2 * tile, total), f32),
        ],
        compiler_params=pltpu.CompilerParams(vmem_limit_bytes=28 * MIB),
        name="analyse",
    )(noise_kind, taper_set, anomaly, seen, other_seen, own_noise, other_noise)

    returned = exchange(increment)

    unpacked = pl.pallas_call(
        unpack_members,
        in_specs=[pl.BlockSpec(memory_space=pltpu.VMEM)],
        out_specs=pl.BlockSpec(memory_space=pltpu.HBM),
        out_shape=jax.ShapeDtypeStruct((members, bands, chunks, LANES), f32),
        scratch_shapes=[
            pltpu.VMEM((members, bands, chunks, LANES), f32),
            pltpu.SemaphoreType.DMA((GROUPS,)),
        ],
        compiler_params=pltpu.CompilerParams(vmem_limit_bytes=12 * MIB),
        name="unpack_members",
    )(returned)
    return unpacked.reshape(members, bands, 1, cells)


def solution(mesh):
    return jax.shard_map(
        shards,
        mesh=mesh,
        in_specs=(
            P("member", None, "region", None),
            P("member", "region", None),
            P("member", "region", None),
            P("member", "region", None, None),
            P("member", None),
            P("member", None),
        ),
        out_specs=P("member", None, "region", None),
        check_vma=False,
    )
```

```python
import jax
import jax.numpy as jnp
from jax import lax
from jax.experimental import pallas as pl
from jax.experimental.pallas import tpu as pltpu
from jax.sharding import PartitionSpec as P

ITERS = 4
TAPER_BASE = 0.7
LANES = 128
GROUPS = 8
COLUMNS = 512
MIB = 1024 * 1024

STRIDE = 21

f32 = jnp.float32
bf16 = jnp.bfloat16


def group_order(devices):
    return [STRIDE * place % devices for place in range(devices)]


def place_of(devices):
    places = [0] * devices
    for place, device in enumerate(group_order(devices)):
        places[device] = place
    return places


def exchange(value):
    order = group_order(value.shape[0])
    return lax.all_to_all(
        value, "member", split_axis=0, concat_axis=0, axis_index_groups=[order], tiled=True
    )


def split3(value):
    high = value.astype(bf16)
    rest = value - high.astype(f32)
    middle = rest.astype(bf16)
    low = (rest - middle.astype(f32)).astype(bf16)
    return high, middle, low


def row_order(rows, members, chunks):
    to = lax.broadcasted_iota(jnp.int32, (rows, rows), 0)
    source = lax.broadcasted_iota(jnp.int32, (rows, rows), 1)
    wanted = lax.rem(to, members) * chunks + lax.div(to, members)
    return jnp.where(source == wanted, 1.0, 0.0).astype(bf16)


def pack_members(x_ref, out_ref, held, arrived):
    members, bands, chunks, lanes = x_ref.shape
    cells = chunks * lanes
    rows = members * chunks
    groups = arrived.shape[0]
    per_group = bands // groups

    def fetch(group):
        span = pl.ds(group * per_group, per_group)
        return pltpu.make_async_copy(x_ref.at[:, span], held.at[:, span], arrived.at[group])

    for group in range(groups):
        fetch(group).start()
    order = row_order(rows, members, chunks)
    place = place_of(bands)
    for group in range(groups):
        fetch(group).wait()
        for pair in range(group * per_group // 2, (group + 1) * per_group // 2):
            parts = []
            for band in (2 * pair, 2 * pair + 1):
                values = held[:, band]
                mean = jnp.sum(values, axis=0) * (1.0 / members)
                high = mean.astype(bf16)
                low = (mean - high.astype(f32)).astype(bf16)
                middle = high.astype(f32) + low.astype(f32)
                out_ref[place[band], :, cells : cells + lanes] = jnp.concatenate([high, low], axis=0)
                parts.append((values - middle[None]).reshape(rows, lanes).astype(bf16))
            moved = jnp.dot(
                order, jnp.concatenate(parts, axis=1), preferred_element_type=f32
            ).astype(bf16)
            for index in range(2):
                for chunk in range(chunks):
                    out_ref[place[2 * pair + index], :, chunk * lanes : (chunk + 1) * lanes] = moved[
                        chunk * members : (chunk + 1) * members,
                        index * lanes : (index + 1) * lanes,
                    ]


def unpack_members(x_ref, out_ref, held, sent):
    bands, members, cells = x_ref.shape
    chunks = cells // LANES
    rows = members * chunks
    groups = sent.shape[0]
    per_group = bands // groups
    order = row_order(rows, chunks, members)
    place = place_of(bands)

    def put(group):
        span = pl.ds(group * per_group, per_group)
        return pltpu.make_async_copy(held.at[:, span], out_ref.at[:, span], sent.at[group])

    for group in range(groups):
        for pair in range(group * per_group // 2, (group + 1) * per_group // 2):
            parts = []
            for band in (2 * pair, 2 * pair + 1):
                parts.append(
                    jnp.concatenate(
                        [
                            x_ref[place[band], :, c * LANES : (c + 1) * LANES]
                            for c in range(chunks)
                        ], axis=0
                    )
                )
            moved = jnp.dot(order, jnp.concatenate(parts, axis=1), preferred_element_type=f32)
            for index in range(2):
                held[:, 2 * pair + index] = moved[
                    :, index * LANES : (index + 1) * LANES
                ].reshape(members, chunks, LANES)
        put(group).start()
    for group in range(groups):
        put(group).wait()


def observe(x_ref, points_ref, readings_ref, anomaly_ref, seen_ref, means, spread, hot):
    sources, members, width = x_ref.shape
    cells = anomaly_ref.shape[1]
    total_members = anomaly_ref.shape[0]
    chunks = cells // LANES
    obs = points_ref.shape[1]

    place = place_of(sources)
    for source in range(sources):
        tail = x_ref[place[source], :, cells:width].astype(f32)
        means[source] = tail[:chunks] + tail[chunks:]
    average = jnp.sum(means[...], axis=0) * (1.0 / sources)

    points = jnp.transpose(jnp.broadcast_to(points_ref[...], (LANES, obs)))
    lane = lax.broadcasted_iota(jnp.int32, (obs, LANES), 1)
    picked = jnp.zeros((obs, LANES), f32)
    for chunk in range(chunks):
        here = points == lane + chunk * LANES
        hot[:, chunk * LANES : (chunk + 1) * LANES] = jnp.where(here, 1.0, 0.0).astype(bf16)
        picked = picked + jnp.where(here, average[chunk : chunk + 1, :], 0.0)
    readings = jnp.transpose(jnp.broadcast_to(readings_ref[...], (LANES, obs)))
    base = readings - jnp.sum(picked, axis=1, keepdims=True)
    high, middle, low = split3(base)
    seen_ref[:, total_members : total_members + LANES] = jnp.where(
        lane == 0, high.astype(f32), jnp.where(lane == 1, middle.astype(f32), low.astype(f32))
    ).astype(bf16)

    spread[...] = means[...] - average[None]

    for source in range(sources):
        rows = slice(source * members, (source + 1) * members)
        shift = spread[source]
        for chunk in range(chunks):
            columns = slice(chunk * LANES, (chunk + 1) * LANES)
            anomaly_ref[rows, columns] = (
                x_ref[place[source], :, columns].astype(f32) + shift[chunk : chunk + 1, :]
            ).astype(bf16)
    for start in range(0, total_members, COLUMNS):
        span = slice(start, start + COLUMNS)
        seen_ref[:, span] = lax.dot_general(
            hot[...],
            anomaly_ref[span, :],
            (((1,), (1,)), ((), ())),
            preferred_element_type=f32,
        ).astype(bf16)


def own_part(anomaly_ref, own_ref, gain_ref, covariance_ref):
    total_members = anomaly_ref.shape[0]
    count = total_members - 1
    rows = own_ref[:, :total_members]
    cross = jnp.dot(rows, anomaly_ref[...], preferred_element_type=f32)
    gain_ref[...] = (cross * (f32(1.0) / count)).astype(bf16)
    product = lax.dot_general(rows, rows, (((1,), (1,)), ((), ())), preferred_element_type=f32)
    covariance_ref[...] = (product * (f32(1.0) / count)).astype(bf16)


def analyse(
    kinds_ref,
    groups_ref,
    anomaly_ref,
    own_ref,
    own_gain_ref,
    own_covariance_ref,
    other_ref,
    own_noise_ref,
    other_noise_ref,
    out_ref,
    seen,
    covariance,
    gain,
    solved,
    zero,
    one_step,
    two_steps,
):
    total_members, cells = anomaly_ref.shape
    tile = own_ref.shape[0]
    rows = 2 * tile
    region = lax.axis_index("region")
    own_kind = kinds_ref[0, region]
    other_kind = kinds_ref[0, 1 - region]
    one = jnp.int32(1)
    own_variance = 0.5 * lax.shift_left(one, own_kind).astype(f32)
    other_variance = 0.5 * lax.shift_left(one, other_kind).astype(f32)
    cross_weight = jnp.where(groups_ref[0, 0] == groups_ref[0, 1], f32(TAPER_BASE), f32(0.0))
    count = total_members - 1

    seen[:tile, :] = own_ref[:, :total_members]
    seen[tile:, :] = other_ref[:, :total_members]
    in_own = lax.broadcasted_iota(jnp.int32, (rows, 1), 0) < tile
    variance = jnp.where(in_own, own_variance, other_variance)

    product = lax.dot_general(
        seen[...], seen[tile:, :], (((1,), (1,)), ((), ())), preferred_element_type=f32
    )
    covariance[:tile, :tile] = own_covariance_ref[...]
    between = product[:tile, :] * (cross_weight / count)
    covariance[:tile, tile:] = between.astype(bf16)
    covariance[tile:, :tile] = jnp.transpose(between).astype(bf16)
    covariance[tile:, tile:] = (product[tile:, :] * (f32(1.0) / count)).astype(bf16)
    bound = variance + jnp.sum(jnp.abs(covariance[...].astype(f32)), axis=1, keepdims=True)
    largest = jnp.max(bound)
    lowest = jnp.minimum(own_variance, other_variance)
    highest = lowest + largest
    center = 0.5 * (highest + lowest)
    radius = 0.5 * (highest - lowest)
    sigma = center / radius
    rho = 1.0 / sigma

    own_base = jnp.sum(own_ref[:, total_members:].astype(f32)[:, :3], axis=1, keepdims=True)
    other_base = jnp.sum(other_ref[:, total_members:].astype(f32)[:, :3], axis=1, keepdims=True)
    own_scale = jnp.sqrt(jnp.full((1, 1), own_variance, f32))
    other_scale = jnp.sqrt(jnp.full((1, 1), other_variance, f32))
    width = COLUMNS

    steps = []
    reach_before, keep_before = 1.0 / center, f32(0.0)
    for _ in range(ITERS - 1):
        rho_next = 1.0 / (2.0 * sigma - rho)
        keep = rho_next * rho
        reach = 2.0 * rho_next / radius
        ratio = reach / reach_before
        steps.append((keep + ratio - reach * variance, ratio * keep_before, reach))
        rho, reach_before, keep_before = rho_next, reach, keep
    inverse = 1.0 / center

    spans = [slice(start, start + width) for start in range(0, total_members, width)]
    for span in spans:
        zero[:tile, span] = inverse * (
            own_base + own_scale * own_noise_ref[:, span].astype(f32) - own_ref[:, span].astype(f32)
        )
        zero[tile:, span] = inverse * (
            other_base
            + other_scale * other_noise_ref[:, span].astype(f32)
            - other_ref[:, span].astype(f32)
        )

    def apply(held, span):
        return jnp.dot(
            covariance[...], held[:, span].astype(bf16), preferred_element_type=f32
        )

    for span in spans:
        ahead, _, reach = steps[0]
        one_step[:, span] = ahead * zero[:, span] - reach * apply(zero, span)
    for span in spans:
        ahead, back, reach = steps[1]
        two_steps[:, span] = (
            ahead * one_step[:, span] - back * zero[:, span] - reach * apply(one_step, span)
        )
    for span in spans:
        ahead, back, reach = steps[2]
        solved[:, span] = (
            (1.0 + ahead) * two_steps[:, span]
            + (1.0 - back) * one_step[:, span]
            + zero[:, span]
            - reach * apply(two_steps, span)
        ).astype(bf16)

    gain[:tile, :] = own_gain_ref[...]
    cross = jnp.dot(seen[tile:, :], anomaly_ref[...], preferred_element_type=f32)
    gain[tile:, :] = (cross * (cross_weight / count)).astype(bf16)
    increment = lax.dot_general(
        solved[...], gain[...], (((0,), (0,)), ((), ())), preferred_element_type=f32
    ).astype(bf16)
    devices, members, _ = out_ref.shape
    for device, place in enumerate(place_of(devices)):
        out_ref[place] = increment[device * members : (device + 1) * members]


def shards(
    prior_samples, measured_point, measured_reading, measurement_noise, noise_kind, taper_set
):
    members, bands, _, cells = prior_samples.shape
    tile = measured_point.shape[2]
    total = measurement_noise.shape[3]
    chunks = cells // LANES
    width = cells + LANES
    swap = [(0, 1), (1, 0)]

    own_noise = measurement_noise.reshape(tile, total)
    other_noise = lax.ppermute(own_noise, "region", swap)

    packed = pl.pallas_call(
        pack_members,
        in_specs=[pl.BlockSpec(memory_space=pltpu.HBM)],
        out_specs=pl.BlockSpec(memory_space=pltpu.VMEM),
        out_shape=jax.ShapeDtypeStruct((bands, members, width), bf16),
        scratch_shapes=[
            pltpu.VMEM((members, bands, chunks, LANES), f32),
            pltpu.SemaphoreType.DMA((GROUPS,)),
        ],
        cost_estimate=pl.CostEstimate(
            flops=4 * members * bands * cells, bytes_accessed=7 * members * bands * cells, transcendentals=0
        ),
        compiler_params=pltpu.CompilerParams(vmem_limit_bytes=50 * MIB),
        name="pack_members",
    )(prior_samples.reshape(members, bands, chunks, LANES))

    packed, other_noise = lax.optimization_barrier((packed, other_noise))
    arrived = exchange(packed)

    anomaly, seen = pl.pallas_call(
        observe,
        in_specs=[pl.BlockSpec(memory_space=pltpu.VMEM)] * 3,
        out_specs=[pl.BlockSpec(memory_space=pltpu.VMEM)] * 2,
        out_shape=[
            jax.ShapeDtypeStruct((total, cells), bf16),
            jax.ShapeDtypeStruct((tile, total + LANES), bf16),
        ],
        scratch_shapes=[
            pltpu.VMEM((bands, chunks, LANES), f32),
            pltpu.VMEM((bands, chunks, LANES), f32),
            pltpu.VMEM((tile, cells), bf16),
        ],
        compiler_params=pltpu.CompilerParams(vmem_limit_bytes=12 * MIB),
        name="observe",
    )(arrived, measured_point.reshape(1, tile), measured_reading.reshape(1, tile))

    other_seen = lax.ppermute(seen, "region", swap)

    own_gain, own_covariance = pl.pallas_call(
        own_part,
        in_specs=[pl.BlockSpec(memory_space=pltpu.VMEM)] * 2,
        out_specs=[pl.BlockSpec(memory_space=pltpu.VMEM)] * 2,
        out_shape=[
            jax.ShapeDtypeStruct((tile, cells), bf16),
            jax.ShapeDtypeStruct((tile, tile), bf16),
        ],
        cost_estimate=pl.CostEstimate(
            flops=2 * tile * total * (cells + tile), bytes_accessed=8 * MIB, transcendentals=0
        ),
        compiler_params=pltpu.CompilerParams(vmem_limit_bytes=12 * MIB),
        name="own_part",
    )(anomaly, seen)

    increment = pl.pallas_call(
        analyse,
        in_specs=[pl.BlockSpec(memory_space=pltpu.SMEM)] * 2
        + [pl.BlockSpec(memory_space=pltpu.VMEM)] * 7,
        out_specs=pl.BlockSpec(memory_space=pltpu.VMEM),
        out_shape=jax.ShapeDtypeStruct((bands, members, cells), bf16),
        scratch_shapes=[
            pltpu.VMEM((2 * tile, total), bf16),
            pltpu.VMEM((2 * tile, 2 * tile), bf16),
            pltpu.VMEM((2 * tile, cells), bf16),
            pltpu.VMEM((2 * tile, total), bf16),
            pltpu.VMEM((2 * tile, total), f32),
            pltpu.VMEM((2 * tile, total), f32),
            pltpu.VMEM((2 * tile, total), f32),
        ],
        compiler_params=pltpu.CompilerParams(vmem_limit_bytes=28 * MIB),
        name="analyse",
    )(
        noise_kind,
        taper_set,
        anomaly,
        seen,
        own_gain,
        own_covariance,
        other_seen,
        own_noise,
        other_noise,
    )

    returned = exchange(increment)

    unpacked = pl.pallas_call(
        unpack_members,
        in_specs=[pl.BlockSpec(memory_space=pltpu.VMEM)],
        out_specs=pl.BlockSpec(memory_space=pltpu.HBM),
        out_shape=jax.ShapeDtypeStruct((members, bands, chunks, LANES), f32),
        scratch_shapes=[
            pltpu.VMEM((members, bands, chunks, LANES), f32),
            pltpu.SemaphoreType.DMA((GROUPS,)),
        ],
        compiler_params=pltpu.CompilerParams(vmem_limit_bytes=12 * MIB),
        name="unpack_members",
    )(returned)
    return unpacked.reshape(members, bands, 1, cells)


def solution(mesh):
    return jax.shard_map(
        shards,
        mesh=mesh,
        in_specs=(
            P("member", None, "region", None),
            P("member", "region", None),
            P("member", "region", None),
            P("member", "region", None, None),
            P("member", None),
            P("member", None),
        ),
        out_specs=P("member", None, "region", None),
        check_vma=False,
    )
```

```python
import jax
import jax.numpy as jnp
from jax import lax
from jax.experimental import pallas as pl
from jax.experimental.pallas import tpu as pltpu
from jax.sharding import PartitionSpec as P

ITERS = 4
TAPER_BASE = 0.7
LANES = 128
GROUPS = 8
COLUMNS = 512
SOLVE_COLUMNS = 256
MIB = 1024 * 1024

STRIDE = 21

f32 = jnp.float32
bf16 = jnp.bfloat16


def group_order(devices):
    return [STRIDE * place % devices for place in range(devices)]


def place_of(devices):
    places = [0] * devices
    for place, device in enumerate(group_order(devices)):
        places[device] = place
    return places


def exchange(value):
    order = group_order(value.shape[0])
    return lax.all_to_all(
        value, "member", split_axis=0, concat_axis=0, axis_index_groups=[order], tiled=True
    )


def split3(value):
    high = value.astype(bf16)
    rest = value - high.astype(f32)
    middle = rest.astype(bf16)
    low = (rest - middle.astype(f32)).astype(bf16)
    return high, middle, low


def row_order(rows, members, chunks):
    to = lax.broadcasted_iota(jnp.int32, (rows, rows), 0)
    source = lax.broadcasted_iota(jnp.int32, (rows, rows), 1)
    wanted = lax.rem(to, members) * chunks + lax.div(to, members)
    return jnp.where(source == wanted, 1.0, 0.0).astype(bf16)


def pack_members(x_ref, out_ref, held, arrived):
    members, bands, chunks, lanes = x_ref.shape
    cells = chunks * lanes
    rows = members * chunks
    groups = arrived.shape[0]
    per_group = bands // groups

    def fetch(group):
        span = pl.ds(group * per_group, per_group)
        return pltpu.make_async_copy(x_ref.at[:, span], held.at[:, span], arrived.at[group])

    for group in range(groups):
        fetch(group).start()
    order = row_order(rows, members, chunks)
    place = place_of(bands)
    for group in range(groups):
        fetch(group).wait()
        for pair in range(group * per_group // 2, (group + 1) * per_group // 2):
            parts = []
            for band in (2 * pair, 2 * pair + 1):
                values = held[:, band]
                mean = jnp.sum(values, axis=0) * (1.0 / members)
                high = mean.astype(bf16)
                low = (mean - high.astype(f32)).astype(bf16)
                middle = high.astype(f32) + low.astype(f32)
                out_ref[place[band], :, cells : cells + lanes] = jnp.concatenate([high, low], axis=0)
                parts.append((values - middle[None]).reshape(rows, lanes).astype(bf16))
            moved = jnp.dot(
                order, jnp.concatenate(parts, axis=1), preferred_element_type=f32
            ).astype(bf16)
            for index in range(2):
                for chunk in range(chunks):
                    out_ref[place[2 * pair + index], :, chunk * lanes : (chunk + 1) * lanes] = moved[
                        chunk * members : (chunk + 1) * members,
                        index * lanes : (index + 1) * lanes,
                    ]


def unpack_members(x_ref, out_ref, held, sent):
    bands, members, cells = x_ref.shape
    chunks = cells // LANES
    rows = members * chunks
    groups = sent.shape[0]
    per_group = bands // groups
    order = row_order(rows, chunks, members)
    place = place_of(bands)

    def put(group):
        span = pl.ds(group * per_group, per_group)
        return pltpu.make_async_copy(held.at[:, span], out_ref.at[:, span], sent.at[group])

    for group in range(groups):
        for pair in range(group * per_group // 2, (group + 1) * per_group // 2):
            parts = []
            for band in (2 * pair, 2 * pair + 1):
                parts.append(
                    jnp.concatenate(
                        [
                            x_ref[place[band], :, c * LANES : (c + 1) * LANES]
                            for c in range(chunks)
                        ], axis=0
                    )
                )
            moved = jnp.dot(order, jnp.concatenate(parts, axis=1), preferred_element_type=f32)
            for index in range(2):
                held[:, 2 * pair + index] = moved[
                    :, index * LANES : (index + 1) * LANES
                ].reshape(members, chunks, LANES)
        put(group).start()
    for group in range(groups):
        put(group).wait()


def observe(x_ref, points_ref, readings_ref, anomaly_ref, seen_ref, means, spread, hot):
    sources, members, width = x_ref.shape
    cells = anomaly_ref.shape[1]
    total_members = anomaly_ref.shape[0]
    chunks = cells // LANES
    obs = points_ref.shape[1]

    place = place_of(sources)
    for source in range(sources):
        tail = x_ref[place[source], :, cells:width].astype(f32)
        means[source] = tail[:chunks] + tail[chunks:]
    average = jnp.sum(means[...], axis=0) * (1.0 / sources)

    points = jnp.transpose(jnp.broadcast_to(points_ref[...], (LANES, obs)))
    lane = lax.broadcasted_iota(jnp.int32, (obs, LANES), 1)
    picked = jnp.zeros((obs, LANES), f32)
    for chunk in range(chunks):
        here = points == lane + chunk * LANES
        hot[:, chunk * LANES : (chunk + 1) * LANES] = jnp.where(here, 1.0, 0.0).astype(bf16)
        picked = picked + jnp.where(here, average[chunk : chunk + 1, :], 0.0)
    readings = jnp.transpose(jnp.broadcast_to(readings_ref[...], (LANES, obs)))
    base = readings - jnp.sum(picked, axis=1, keepdims=True)
    high, middle, low = split3(base)
    seen_ref[:, total_members : total_members + LANES] = jnp.where(
        lane == 0, high.astype(f32), jnp.where(lane == 1, middle.astype(f32), low.astype(f32))
    ).astype(bf16)

    spread[...] = means[...] - average[None]

    for source in range(sources):
        rows = slice(source * members, (source + 1) * members)
        shift = spread[source]
        for chunk in range(chunks):
            columns = slice(chunk * LANES, (chunk + 1) * LANES)
            anomaly_ref[rows, columns] = (
                x_ref[place[source], :, columns].astype(f32) + shift[chunk : chunk + 1, :]
            ).astype(bf16)
    for start in range(0, total_members, COLUMNS):
        span = slice(start, start + COLUMNS)
        seen_ref[:, span] = lax.dot_general(
            hot[...],
            anomaly_ref[span, :],
            (((1,), (1,)), ((), ())),
            preferred_element_type=f32,
        ).astype(bf16)


def own_part(anomaly_ref, own_ref, gain_ref, covariance_ref):
    total_members = anomaly_ref.shape[0]
    count = total_members - 1
    rows = own_ref[:, :total_members]
    cross = jnp.dot(rows, anomaly_ref[...], preferred_element_type=f32)
    gain_ref[...] = (cross * (f32(1.0) / count)).astype(bf16)
    product = lax.dot_general(rows, rows, (((1,), (1,)), ((), ())), preferred_element_type=f32)
    covariance_ref[...] = (product * (f32(1.0) / count)).astype(bf16)


def analyse(
    kinds_ref,
    groups_ref,
    anomaly_ref,
    own_ref,
    own_gain_ref,
    own_covariance_ref,
    other_ref,
    own_noise_ref,
    other_noise_ref,
    out_ref,
    seen,
    covariance,
    gain,
    solved,
    zero,
    one_step,
    two_steps,
):
    total_members, cells = anomaly_ref.shape
    tile = own_ref.shape[0]
    rows = 2 * tile
    region = lax.axis_index("region")
    own_kind = kinds_ref[0, region]
    other_kind = kinds_ref[0, 1 - region]
    one = jnp.int32(1)
    own_variance = 0.5 * lax.shift_left(one, own_kind).astype(f32)
    other_variance = 0.5 * lax.shift_left(one, other_kind).astype(f32)
    cross_weight = jnp.where(groups_ref[0, 0] == groups_ref[0, 1], f32(TAPER_BASE), f32(0.0))
    count = total_members - 1

    seen[:tile, :] = own_ref[:, :total_members]
    seen[tile:, :] = other_ref[:, :total_members]
    in_own = lax.broadcasted_iota(jnp.int32, (rows, 1), 0) < tile
    variance = jnp.where(in_own, own_variance, other_variance)

    product = lax.dot_general(
        seen[...], seen[tile:, :], (((1,), (1,)), ((), ())), preferred_element_type=f32
    )
    covariance[:tile, :tile] = own_covariance_ref[...]
    between = product[:tile, :] * (cross_weight / count)
    covariance[:tile, tile:] = between.astype(bf16)
    covariance[tile:, :tile] = jnp.transpose(between).astype(bf16)
    covariance[tile:, tile:] = (product[tile:, :] * (f32(1.0) / count)).astype(bf16)
    bound = variance + jnp.sum(jnp.abs(covariance[...].astype(f32)), axis=1, keepdims=True)
    largest = jnp.max(bound)
    lowest = jnp.minimum(own_variance, other_variance)
    highest = lowest + largest
    center = 0.5 * (highest + lowest)
    radius = 0.5 * (highest - lowest)
    sigma = center / radius
    rho = 1.0 / sigma

    own_base = jnp.sum(own_ref[:, total_members:].astype(f32)[:, :3], axis=1, keepdims=True)
    other_base = jnp.sum(other_ref[:, total_members:].astype(f32)[:, :3], axis=1, keepdims=True)
    own_scale = jnp.sqrt(jnp.full((1, 1), own_variance, f32))
    other_scale = jnp.sqrt(jnp.full((1, 1), other_variance, f32))
    width = SOLVE_COLUMNS

    steps = []
    reach_before, keep_before = 1.0 / center, f32(0.0)
    for _ in range(ITERS - 1):
        rho_next = 1.0 / (2.0 * sigma - rho)
        keep = rho_next * rho
        reach = 2.0 * rho_next / radius
        ratio = reach / reach_before
        steps.append((keep + ratio - reach * variance, ratio * keep_before, reach))
        rho, reach_before, keep_before = rho_next, reach, keep
    inverse = 1.0 / center

    spans = [slice(left, left + width) for left in range(0, total_members, width)]
    devices, members, _ = out_ref.shape
    places = place_of(devices)

    def apply(held, span):
        return jnp.dot(
            covariance[...], held[:, span].astype(bf16), preferred_element_type=f32
        )

    def settle(span):
        ahead, back, reach = steps[2]
        solved[:, span] = (
            (1.0 + ahead) * two_steps[:, span]
            + (1.0 - back) * one_step[:, span]
            + zero[:, span]
            - reach * apply(two_steps, span)
        ).astype(bf16)

    def finish(span):
        part = lax.dot_general(
            solved[:, span], gain[...], (((0,), (0,)), ((), ())), preferred_element_type=f32
        ).astype(bf16)
        for device in range(span.start // members, span.stop // members):
            first = device * members - span.start
            out_ref[places[device]] = part[first : first + members]

    for span in spans:
        zero[:tile, span] = inverse * (
            own_base + own_scale * own_noise_ref[:, span].astype(f32) - own_ref[:, span].astype(f32)
        )
        zero[tile:, span] = inverse * (
            other_base
            + other_scale * other_noise_ref[:, span].astype(f32)
            - other_ref[:, span].astype(f32)
        )
    gain[:tile, :] = own_gain_ref[...]
    cross = jnp.dot(seen[tile:, :], anomaly_ref[...], preferred_element_type=f32)
    gain[tile:, :] = (cross * (cross_weight / count)).astype(bf16)
    for span in spans:
        ahead, _, reach = steps[0]
        one_step[:, span] = ahead * zero[:, span] - reach * apply(zero, span)
    for span in spans:
        ahead, back, reach = steps[1]
        two_steps[:, span] = (
            ahead * one_step[:, span] - back * zero[:, span] - reach * apply(one_step, span)
        )
    settle(spans[0])
    for span, later in zip(spans, spans[1:]):
        settle(later)
        finish(span)
    finish(spans[-1])


def shards(
    prior_samples, measured_point, measured_reading, measurement_noise, noise_kind, taper_set
):
    members, bands, _, cells = prior_samples.shape
    tile = measured_point.shape[2]
    total = measurement_noise.shape[3]
    chunks = cells // LANES
    width = cells + LANES
    swap = [(0, 1), (1, 0)]

    own_noise = measurement_noise.reshape(tile, total)
    other_noise = lax.ppermute(own_noise, "region", swap)

    packed = pl.pallas_call(
        pack_members,
        in_specs=[pl.BlockSpec(memory_space=pltpu.HBM)],
        out_specs=pl.BlockSpec(memory_space=pltpu.VMEM),
        out_shape=jax.ShapeDtypeStruct((bands, members, width), bf16),
        scratch_shapes=[
            pltpu.VMEM((members, bands, chunks, LANES), f32),
            pltpu.SemaphoreType.DMA((GROUPS,)),
        ],
        cost_estimate=pl.CostEstimate(
            flops=4 * members * bands * cells, bytes_accessed=7 * members * bands * cells, transcendentals=0
        ),
        compiler_params=pltpu.CompilerParams(vmem_limit_bytes=50 * MIB),
        name="pack_members",
    )(prior_samples.reshape(members, bands, chunks, LANES))

    packed, other_noise = lax.optimization_barrier((packed, other_noise))
    arrived = exchange(packed)

    anomaly, seen = pl.pallas_call(
        observe,
        in_specs=[pl.BlockSpec(memory_space=pltpu.VMEM)] * 3,
        out_specs=[pl.BlockSpec(memory_space=pltpu.VMEM)] * 2,
        out_shape=[
            jax.ShapeDtypeStruct((total, cells), bf16),
            jax.ShapeDtypeStruct((tile, total + LANES), bf16),
        ],
        scratch_shapes=[
            pltpu.VMEM((bands, chunks, LANES), f32),
            pltpu.VMEM((bands, chunks, LANES), f32),
            pltpu.VMEM((tile, cells), bf16),
        ],
        compiler_params=pltpu.CompilerParams(vmem_limit_bytes=12 * MIB),
        name="observe",
    )(arrived, measured_point.reshape(1, tile), measured_reading.reshape(1, tile))

    other_seen = lax.ppermute(seen, "region", swap)

    own_gain, own_covariance = pl.pallas_call(
        own_part,
        in_specs=[pl.BlockSpec(memory_space=pltpu.VMEM)] * 2,
        out_specs=[pl.BlockSpec(memory_space=pltpu.VMEM)] * 2,
        out_shape=[
            jax.ShapeDtypeStruct((tile, cells), bf16),
            jax.ShapeDtypeStruct((tile, tile), bf16),
        ],
        cost_estimate=pl.CostEstimate(
            flops=2 * tile * total * (cells + tile), bytes_accessed=8 * MIB, transcendentals=0
        ),
        compiler_params=pltpu.CompilerParams(vmem_limit_bytes=12 * MIB),
        name="own_part",
    )(anomaly, seen)

    increment = pl.pallas_call(
        analyse,
        in_specs=[pl.BlockSpec(memory_space=pltpu.SMEM)] * 2
        + [pl.BlockSpec(memory_space=pltpu.VMEM)] * 7,
        out_specs=pl.BlockSpec(memory_space=pltpu.VMEM),
        out_shape=jax.ShapeDtypeStruct((bands, members, cells), bf16),
        scratch_shapes=[
            pltpu.VMEM((2 * tile, total), bf16),
            pltpu.VMEM((2 * tile, 2 * tile), bf16),
            pltpu.VMEM((2 * tile, cells), bf16),
            pltpu.VMEM((2 * tile, total), bf16),
            pltpu.VMEM((2 * tile, total), f32),
            pltpu.VMEM((2 * tile, total), f32),
            pltpu.VMEM((2 * tile, total), f32),
        ],
        compiler_params=pltpu.CompilerParams(vmem_limit_bytes=28 * MIB),
        name="analyse",
    )(
        noise_kind,
        taper_set,
        anomaly,
        seen,
        own_gain,
        own_covariance,
        other_seen,
        own_noise,
        other_noise,
    )

    returned = exchange(increment)

    unpacked = pl.pallas_call(
        unpack_members,
        in_specs=[pl.BlockSpec(memory_space=pltpu.VMEM)],
        out_specs=pl.BlockSpec(memory_space=pltpu.HBM),
        out_shape=jax.ShapeDtypeStruct((members, bands, chunks, LANES), f32),
        scratch_shapes=[
            pltpu.VMEM((members, bands, chunks, LANES), f32),
            pltpu.SemaphoreType.DMA((GROUPS,)),
        ],
        compiler_params=pltpu.CompilerParams(vmem_limit_bytes=12 * MIB),
        name="unpack_members",
    )(returned)
    return unpacked.reshape(members, bands, 1, cells)


def solution(mesh):
    return jax.shard_map(
        shards,
        mesh=mesh,
        in_specs=(
            P("member", None, "region", None),
            P("member", "region", None),
            P("member", "region", None),
            P("member", "region", None, None),
            P("member", None),
            P("member", None),
        ),
        out_specs=P("member", None, "region", None),
        check_vma=False,
    )
```

```python
import jax
import jax.numpy as jnp
from jax import lax
from jax.experimental import pallas as pl
from jax.experimental.pallas import tpu as pltpu
from jax.sharding import PartitionSpec as P

ITERS = 4
TAPER_BASE = 0.7
LANES = 128
GROUPS = 8
COLUMNS = 512
SOLVE_COLUMNS = 256
MIB = 1024 * 1024

STRIDE = 21

f32 = jnp.float32
bf16 = jnp.bfloat16


def group_order(devices):
    return [STRIDE * place % devices for place in range(devices)]


def place_of(devices):
    places = [0] * devices
    for place, device in enumerate(group_order(devices)):
        places[device] = place
    return places


def exchange(value):
    order = group_order(value.shape[0])
    return lax.all_to_all(
        value, "member", split_axis=0, concat_axis=0, axis_index_groups=[order], tiled=True
    )


def split3(value):
    high = value.astype(bf16)
    rest = value - high.astype(f32)
    middle = rest.astype(bf16)
    low = (rest - middle.astype(f32)).astype(bf16)
    return high, middle, low


def row_order(rows, members, chunks):
    to = lax.broadcasted_iota(jnp.int32, (rows, rows), 0)
    source = lax.broadcasted_iota(jnp.int32, (rows, rows), 1)
    wanted = lax.rem(to, members) * chunks + lax.div(to, members)
    return jnp.where(source == wanted, 1.0, 0.0).astype(bf16)


def pack_members(x_ref, out_ref, held, arrived):
    members, bands, chunks, lanes = x_ref.shape
    cells = chunks * lanes
    rows = members * chunks
    groups = arrived.shape[0]
    per_group = bands // groups

    def fetch(group):
        span = pl.ds(group * per_group, per_group)
        return pltpu.make_async_copy(x_ref.at[:, span], held.at[:, span], arrived.at[group])

    for group in range(groups):
        fetch(group).start()
    order = row_order(rows, members, chunks)
    place = place_of(bands)
    for group in range(groups):
        fetch(group).wait()
        for pair in range(group * per_group // 2, (group + 1) * per_group // 2):
            parts = []
            for band in (2 * pair, 2 * pair + 1):
                values = held[:, band]
                mean = jnp.sum(values, axis=0) * (1.0 / members)
                high = mean.astype(bf16)
                low = (mean - high.astype(f32)).astype(bf16)
                middle = high.astype(f32) + low.astype(f32)
                out_ref[place[band], :, cells : cells + lanes] = jnp.concatenate([high, low], axis=0)
                parts.append((values - middle[None]).reshape(rows, lanes).astype(bf16))
            moved = jnp.dot(
                order, jnp.concatenate(parts, axis=1), preferred_element_type=f32
            ).astype(bf16)
            for index in range(2):
                for chunk in range(chunks):
                    out_ref[place[2 * pair + index], :, chunk * lanes : (chunk + 1) * lanes] = moved[
                        chunk * members : (chunk + 1) * members,
                        index * lanes : (index + 1) * lanes,
                    ]


def unpack_members(x_ref, out_ref, held, sent):
    bands, members, cells = x_ref.shape
    chunks = cells // LANES
    rows = members * chunks
    groups = sent.shape[0]
    per_group = bands // groups
    order = row_order(rows, chunks, members)
    place = place_of(bands)

    def put(group):
        span = pl.ds(group * per_group, per_group)
        return pltpu.make_async_copy(held.at[:, span], out_ref.at[:, span], sent.at[group])

    for group in range(groups):
        for pair in range(group * per_group // 2, (group + 1) * per_group // 2):
            parts = []
            for band in (2 * pair, 2 * pair + 1):
                parts.append(
                    jnp.concatenate(
                        [
                            x_ref[place[band], :, c * LANES : (c + 1) * LANES]
                            for c in range(chunks)
                        ], axis=0
                    )
                )
            moved = jnp.dot(order, jnp.concatenate(parts, axis=1), preferred_element_type=f32)
            for index in range(2):
                held[:, 2 * pair + index] = moved[
                    :, index * LANES : (index + 1) * LANES
                ].reshape(members, chunks, LANES)
        put(group).start()
    for group in range(groups):
        put(group).wait()


def observe(x_ref, points_ref, readings_ref, anomaly_ref, seen_ref, means, spread, hot):
    sources, members, width = x_ref.shape
    cells = anomaly_ref.shape[1]
    total_members = anomaly_ref.shape[0]
    chunks = cells // LANES
    obs = points_ref.shape[1]

    place = place_of(sources)
    for source in range(sources):
        tail = x_ref[place[source], :, cells:width].astype(f32)
        means[source] = tail[:chunks] + tail[chunks:]
    average = jnp.sum(means[...], axis=0) * (1.0 / sources)

    points = jnp.transpose(jnp.broadcast_to(points_ref[...], (LANES, obs)))
    lane = lax.broadcasted_iota(jnp.int32, (obs, LANES), 1)
    picked = jnp.zeros((obs, LANES), f32)
    for chunk in range(chunks):
        here = points == lane + chunk * LANES
        hot[:, chunk * LANES : (chunk + 1) * LANES] = jnp.where(here, 1.0, 0.0).astype(bf16)
        picked = picked + jnp.where(here, average[chunk : chunk + 1, :], 0.0)
    readings = jnp.transpose(jnp.broadcast_to(readings_ref[...], (LANES, obs)))
    base = readings - jnp.sum(picked, axis=1, keepdims=True)
    high, middle, low = split3(base)
    seen_ref[:, total_members : total_members + LANES] = jnp.where(
        lane == 0, high.astype(f32), jnp.where(lane == 1, middle.astype(f32), low.astype(f32))
    ).astype(bf16)

    spread[...] = means[...] - average[None]

    for source in range(sources):
        rows = slice(source * members, (source + 1) * members)
        shift = spread[source]
        for chunk in range(chunks):
            columns = slice(chunk * LANES, (chunk + 1) * LANES)
            anomaly_ref[rows, columns] = (
                x_ref[place[source], :, columns].astype(f32) + shift[chunk : chunk + 1, :]
            ).astype(bf16)
    for start in range(0, total_members, COLUMNS):
        span = slice(start, start + COLUMNS)
        seen_ref[:, span] = lax.dot_general(
            hot[...],
            anomaly_ref[span, :],
            (((1,), (1,)), ((), ())),
            preferred_element_type=f32,
        ).astype(bf16)


def own_part(
    kinds_ref, anomaly_ref, own_ref, noise_ref, gain_ref, covariance_ref, innovation_ref
):
    total_members = anomaly_ref.shape[0]
    count = total_members - 1
    rows = own_ref[:, :total_members]
    cross = jnp.dot(rows, anomaly_ref[...], preferred_element_type=f32)
    gain_ref[...] = (cross * (f32(1.0) / count)).astype(bf16)
    product = lax.dot_general(rows, rows, (((1,), (1,)), ((), ())), preferred_element_type=f32)
    covariance_ref[...] = (product * (f32(1.0) / count)).astype(bf16)
    kind = kinds_ref[0, lax.axis_index("region")]
    variance = 0.5 * lax.shift_left(jnp.int32(1), kind).astype(f32)
    scale = jnp.sqrt(jnp.full((1, 1), variance, f32))
    base = jnp.sum(own_ref[:, total_members:].astype(f32)[:, :3], axis=1, keepdims=True)
    innovation_ref[...] = base + scale * noise_ref[...].astype(f32) - rows.astype(f32)


def analyse(
    kinds_ref,
    groups_ref,
    anomaly_ref,
    own_ref,
    own_gain_ref,
    own_covariance_ref,
    other_ref,
    own_innovation_ref,
    other_noise_ref,
    out_ref,
    seen,
    covariance,
    gain,
    solved,
    zero,
    one_step,
    two_steps,
):
    total_members, cells = anomaly_ref.shape
    tile = own_ref.shape[0]
    rows = 2 * tile
    region = lax.axis_index("region")
    own_kind = kinds_ref[0, region]
    other_kind = kinds_ref[0, 1 - region]
    one = jnp.int32(1)
    own_variance = 0.5 * lax.shift_left(one, own_kind).astype(f32)
    other_variance = 0.5 * lax.shift_left(one, other_kind).astype(f32)
    cross_weight = jnp.where(groups_ref[0, 0] == groups_ref[0, 1], f32(TAPER_BASE), f32(0.0))
    count = total_members - 1

    seen[:tile, :] = own_ref[:, :total_members]
    seen[tile:, :] = other_ref[:, :total_members]
    in_own = lax.broadcasted_iota(jnp.int32, (rows, 1), 0) < tile
    variance = jnp.where(in_own, own_variance, other_variance)

    product = lax.dot_general(
        seen[...], seen[tile:, :], (((1,), (1,)), ((), ())), preferred_element_type=f32
    )
    covariance[:tile, :tile] = own_covariance_ref[...]
    between = product[:tile, :] * (cross_weight / count)
    covariance[:tile, tile:] = between.astype(bf16)
    covariance[tile:, :tile] = jnp.transpose(between).astype(bf16)
    covariance[tile:, tile:] = (product[tile:, :] * (f32(1.0) / count)).astype(bf16)
    bound = variance + jnp.sum(jnp.abs(covariance[...].astype(f32)), axis=1, keepdims=True)
    largest = jnp.max(bound)
    lowest = jnp.minimum(own_variance, other_variance)
    highest = lowest + largest
    center = 0.5 * (highest + lowest)
    radius = 0.5 * (highest - lowest)
    sigma = center / radius
    rho = 1.0 / sigma

    other_base = jnp.sum(other_ref[:, total_members:].astype(f32)[:, :3], axis=1, keepdims=True)
    other_scale = jnp.sqrt(jnp.full((1, 1), other_variance, f32))
    width = SOLVE_COLUMNS

    steps = []
    reach_before, keep_before = 1.0 / center, f32(0.0)
    for _ in range(ITERS - 1):
        rho_next = 1.0 / (2.0 * sigma - rho)
        keep = rho_next * rho
        reach = 2.0 * rho_next / radius
        ratio = reach / reach_before
        steps.append((keep + ratio - reach * variance, ratio * keep_before, reach))
        rho, reach_before, keep_before = rho_next, reach, keep
    inverse = 1.0 / center

    spans = [slice(left, left + width) for left in range(0, total_members, width)]
    devices, members, _ = out_ref.shape
    places = place_of(devices)

    def apply(held, span):
        return jnp.dot(
            covariance[...], held[:, span].astype(bf16), preferred_element_type=f32
        )

    def settle(span):
        ahead, back, reach = steps[2]
        solved[:, span] = (
            (1.0 + ahead) * two_steps[:, span]
            + (1.0 - back) * one_step[:, span]
            + zero[:, span]
            - reach * apply(two_steps, span)
        ).astype(bf16)

    def finish(span):
        part = lax.dot_general(
            solved[:, span], gain[...], (((0,), (0,)), ((), ())), preferred_element_type=f32
        ).astype(bf16)
        for device in range(span.start // members, span.stop // members):
            first = device * members - span.start
            out_ref[places[device]] = part[first : first + members]

    for span in spans:
        zero[:tile, span] = inverse * own_innovation_ref[:, span]
        zero[tile:, span] = inverse * (
            other_base
            + other_scale * other_noise_ref[:, span].astype(f32)
            - other_ref[:, span].astype(f32)
        )
    gain[:tile, :] = own_gain_ref[...]
    cross = jnp.dot(seen[tile:, :], anomaly_ref[...], preferred_element_type=f32)
    gain[tile:, :] = (cross * (cross_weight / count)).astype(bf16)
    for span in spans:
        ahead, _, reach = steps[0]
        one_step[:, span] = ahead * zero[:, span] - reach * apply(zero, span)
    for span in spans:
        ahead, back, reach = steps[1]
        two_steps[:, span] = (
            ahead * one_step[:, span] - back * zero[:, span] - reach * apply(one_step, span)
        )
    settle(spans[0])
    for span, later in zip(spans, spans[1:]):
        settle(later)
        finish(span)
    finish(spans[-1])


def shards(
    prior_samples, measured_point, measured_reading, measurement_noise, noise_kind, taper_set
):
    members, bands, _, cells = prior_samples.shape
    tile = measured_point.shape[2]
    total = measurement_noise.shape[3]
    chunks = cells // LANES
    width = cells + LANES
    swap = [(0, 1), (1, 0)]

    own_noise = measurement_noise.reshape(tile, total)
    other_noise = lax.ppermute(own_noise, "region", swap)

    packed = pl.pallas_call(
        pack_members,
        in_specs=[pl.BlockSpec(memory_space=pltpu.HBM)],
        out_specs=pl.BlockSpec(memory_space=pltpu.VMEM),
        out_shape=jax.ShapeDtypeStruct((bands, members, width), bf16),
        scratch_shapes=[
            pltpu.VMEM((members, bands, chunks, LANES), f32),
            pltpu.SemaphoreType.DMA((GROUPS,)),
        ],
        cost_estimate=pl.CostEstimate(
            flops=4 * members * bands * cells, bytes_accessed=7 * members * bands * cells, transcendentals=0
        ),
        compiler_params=pltpu.CompilerParams(vmem_limit_bytes=50 * MIB),
        name="pack_members",
    )(prior_samples.reshape(members, bands, chunks, LANES))

    packed, other_noise = lax.optimization_barrier((packed, other_noise))
    arrived = exchange(packed)

    anomaly, seen = pl.pallas_call(
        observe,
        in_specs=[pl.BlockSpec(memory_space=pltpu.VMEM)] * 3,
        out_specs=[pl.BlockSpec(memory_space=pltpu.VMEM)] * 2,
        out_shape=[
            jax.ShapeDtypeStruct((total, cells), bf16),
            jax.ShapeDtypeStruct((tile, total + LANES), bf16),
        ],
        scratch_shapes=[
            pltpu.VMEM((bands, chunks, LANES), f32),
            pltpu.VMEM((bands, chunks, LANES), f32),
            pltpu.VMEM((tile, cells), bf16),
        ],
        compiler_params=pltpu.CompilerParams(vmem_limit_bytes=12 * MIB),
        name="observe",
    )(arrived, measured_point.reshape(1, tile), measured_reading.reshape(1, tile))

    other_seen = lax.ppermute(seen, "region", swap)

    own_gain, own_covariance, own_innovation = pl.pallas_call(
        own_part,
        in_specs=[pl.BlockSpec(memory_space=pltpu.SMEM)]
        + [pl.BlockSpec(memory_space=pltpu.VMEM)] * 3,
        out_specs=[pl.BlockSpec(memory_space=pltpu.VMEM)] * 3,
        out_shape=[
            jax.ShapeDtypeStruct((tile, cells), bf16),
            jax.ShapeDtypeStruct((tile, tile), bf16),
            jax.ShapeDtypeStruct((tile, total), f32),
        ],
        cost_estimate=pl.CostEstimate(
            flops=2 * tile * total * (cells + tile), bytes_accessed=8 * MIB, transcendentals=0
        ),
        compiler_params=pltpu.CompilerParams(vmem_limit_bytes=12 * MIB),
        name="own_part",
    )(noise_kind, anomaly, seen, own_noise)

    increment = pl.pallas_call(
        analyse,
        in_specs=[pl.BlockSpec(memory_space=pltpu.SMEM)] * 2
        + [pl.BlockSpec(memory_space=pltpu.VMEM)] * 7,
        out_specs=pl.BlockSpec(memory_space=pltpu.VMEM),
        out_shape=jax.ShapeDtypeStruct((bands, members, cells), bf16),
        scratch_shapes=[
            pltpu.VMEM((2 * tile, total), bf16),
            pltpu.VMEM((2 * tile, 2 * tile), bf16),
            pltpu.VMEM((2 * tile, cells), bf16),
            pltpu.VMEM((2 * tile, total), bf16),
            pltpu.VMEM((2 * tile, total), f32),
            pltpu.VMEM((2 * tile, total), f32),
            pltpu.VMEM((2 * tile, total), f32),
        ],
        compiler_params=pltpu.CompilerParams(vmem_limit_bytes=28 * MIB),
        name="analyse",
    )(
        noise_kind,
        taper_set,
        anomaly,
        seen,
        own_gain,
        own_covariance,
        other_seen,
        own_innovation,
        other_noise,
    )

    returned = exchange(increment)

    unpacked = pl.pallas_call(
        unpack_members,
        in_specs=[pl.BlockSpec(memory_space=pltpu.VMEM)],
        out_specs=pl.BlockSpec(memory_space=pltpu.HBM),
        out_shape=jax.ShapeDtypeStruct((members, bands, chunks, LANES), f32),
        scratch_shapes=[
            pltpu.VMEM((members, bands, chunks, LANES), f32),
            pltpu.SemaphoreType.DMA((GROUPS,)),
        ],
        compiler_params=pltpu.CompilerParams(vmem_limit_bytes=12 * MIB),
        name="unpack_members",
    )(returned)
    return unpacked.reshape(members, bands, 1, cells)


def solution(mesh):
    return jax.shard_map(
        shards,
        mesh=mesh,
        in_specs=(
            P("member", None, "region", None),
            P("member", "region", None),
            P("member", "region", None),
            P("member", "region", None, None),
            P("member", None),
            P("member", None),
        ),
        out_specs=P("member", None, "region", None),
        check_vma=False,
    )
```

```python
import jax
import jax.numpy as jnp
from jax import lax
from jax.experimental import pallas as pl
from jax.experimental.pallas import tpu as pltpu
from jax.sharding import PartitionSpec as P

ITERS = 4
TAPER_BASE = 0.7
LANES = 128
GROUPS = 8
COLUMNS = 512
SOLVE_COLUMNS = 256
MIB = 1024 * 1024

STRIDE = 21

f32 = jnp.float32
bf16 = jnp.bfloat16


def group_order(devices):
    return [STRIDE * place % devices for place in range(devices)]


def place_of(devices):
    places = [0] * devices
    for place, device in enumerate(group_order(devices)):
        places[device] = place
    return places


def exchange(value):
    order = group_order(value.shape[0])
    return lax.all_to_all(
        value, "member", split_axis=0, concat_axis=0, axis_index_groups=[order], tiled=True
    )


def split3(value):
    high = value.astype(bf16)
    rest = value - high.astype(f32)
    middle = rest.astype(bf16)
    low = (rest - middle.astype(f32)).astype(bf16)
    return high, middle, low


def row_order(rows, members, chunks):
    to = lax.broadcasted_iota(jnp.int32, (rows, rows), 0)
    source = lax.broadcasted_iota(jnp.int32, (rows, rows), 1)
    wanted = lax.rem(to, members) * chunks + lax.div(to, members)
    return jnp.where(source == wanted, 1.0, 0.0).astype(bf16)


def pack_members(x_ref, out_ref, held, arrived):
    members, bands, chunks, lanes = x_ref.shape
    cells = chunks * lanes
    rows = members * chunks
    groups = arrived.shape[0]
    per_group = bands // groups

    def fetch(group):
        span = pl.ds(group * per_group, per_group)
        return pltpu.make_async_copy(x_ref.at[:, span], held.at[:, span], arrived.at[group])

    for group in range(groups):
        fetch(group).start()
    order = row_order(rows, members, chunks)
    place = place_of(bands)
    for group in range(groups):
        fetch(group).wait()
        for pair in range(group * per_group // 2, (group + 1) * per_group // 2):
            parts = []
            for band in (2 * pair, 2 * pair + 1):
                values = held[:, band]
                mean = jnp.sum(values, axis=0) * (1.0 / members)
                high = mean.astype(bf16)
                low = (mean - high.astype(f32)).astype(bf16)
                middle = high.astype(f32) + low.astype(f32)
                out_ref[place[band], :, cells : cells + lanes] = jnp.concatenate([high, low], axis=0)
                parts.append((values - middle[None]).reshape(rows, lanes).astype(bf16))
            moved = jnp.dot(
                order, jnp.concatenate(parts, axis=1), preferred_element_type=f32
            ).astype(bf16)
            for index in range(2):
                for chunk in range(chunks):
                    out_ref[place[2 * pair + index], :, chunk * lanes : (chunk + 1) * lanes] = moved[
                        chunk * members : (chunk + 1) * members,
                        index * lanes : (index + 1) * lanes,
                    ]


def unpack_members(x_ref, out_ref, held, sent):
    bands, members, cells = x_ref.shape
    chunks = cells // LANES
    rows = members * chunks
    groups = sent.shape[0]
    per_group = bands // groups
    order = row_order(rows, chunks, members)
    place = place_of(bands)

    def put(group):
        span = pl.ds(group * per_group, per_group)
        return pltpu.make_async_copy(held.at[:, span], out_ref.at[:, span], sent.at[group])

    for group in range(groups):
        for pair in range(group * per_group // 2, (group + 1) * per_group // 2):
            parts = []
            for band in (2 * pair, 2 * pair + 1):
                parts.append(
                    jnp.concatenate(
                        [
                            x_ref[place[band], :, c * LANES : (c + 1) * LANES]
                            for c in range(chunks)
                        ], axis=0
                    )
                )
            moved = jnp.dot(order, jnp.concatenate(parts, axis=1), preferred_element_type=f32)
            for index in range(2):
                held[:, 2 * pair + index] = moved[
                    :, index * LANES : (index + 1) * LANES
                ].reshape(members, chunks, LANES)
        put(group).start()
    for group in range(groups):
        put(group).wait()


def observe(x_ref, points_ref, readings_ref, anomaly_ref, seen_ref, means, spread, hot):
    sources, members, width = x_ref.shape
    cells = anomaly_ref.shape[1]
    total_members = anomaly_ref.shape[0]
    chunks = cells // LANES
    obs = points_ref.shape[1]

    place = place_of(sources)
    for source in range(sources):
        tail = x_ref[place[source], :, cells:width].astype(f32)
        means[source] = tail[:chunks] + tail[chunks:]
    average = jnp.sum(means[...], axis=0) * (1.0 / sources)

    points = jnp.transpose(jnp.broadcast_to(points_ref[...], (LANES, obs)))
    lane = lax.broadcasted_iota(jnp.int32, (obs, LANES), 1)
    picked = jnp.zeros((obs, LANES), f32)
    for chunk in range(chunks):
        here = points == lane + chunk * LANES
        hot[:, chunk * LANES : (chunk + 1) * LANES] = jnp.where(here, 1.0, 0.0).astype(bf16)
        picked = picked + jnp.where(here, average[chunk : chunk + 1, :], 0.0)
    readings = jnp.transpose(jnp.broadcast_to(readings_ref[...], (LANES, obs)))
    base = readings - jnp.sum(picked, axis=1, keepdims=True)
    high, middle, low = split3(base)
    seen_ref[:, total_members : total_members + LANES] = jnp.where(
        lane == 0, high.astype(f32), jnp.where(lane == 1, middle.astype(f32), low.astype(f32))
    ).astype(bf16)

    spread[...] = means[...] - average[None]

    for source in range(sources):
        rows = slice(source * members, (source + 1) * members)
        shift = spread[source]
        for chunk in range(chunks):
            columns = slice(chunk * LANES, (chunk + 1) * LANES)
            anomaly_ref[rows, columns] = (
                x_ref[place[source], :, columns].astype(f32) + shift[chunk : chunk + 1, :]
            ).astype(bf16)
    for start in range(0, total_members, COLUMNS):
        span = slice(start, start + COLUMNS)
        seen_ref[:, span] = lax.dot_general(
            hot[...],
            anomaly_ref[span, :],
            (((1,), (1,)), ((), ())),
            preferred_element_type=f32,
        ).astype(bf16)


def own_part(anomaly_ref, own_ref, gain_ref, covariance_ref):
    total_members = anomaly_ref.shape[0]
    count = total_members - 1
    rows = own_ref[:, :total_members]
    cross = jnp.dot(rows, anomaly_ref[...], preferred_element_type=f32)
    gain_ref[...] = (cross * (f32(1.0) / count)).astype(bf16)
    product = lax.dot_general(rows, rows, (((1,), (1,)), ((), ())), preferred_element_type=f32)
    covariance_ref[...] = (product * (f32(1.0) / count)).astype(bf16)


def analyse(
    kinds_ref,
    groups_ref,
    anomaly_ref,
    own_ref,
    own_gain_ref,
    own_covariance_ref,
    other_ref,
    own_noise_ref,
    other_noise_ref,
    out_ref,
    seen,
    covariance,
    gain,
    solved,
    zero,
    one_step,
    two_steps,
):
    total_members, cells = anomaly_ref.shape
    tile = own_ref.shape[0]
    rows = 2 * tile
    region = lax.axis_index("region")
    own_kind = kinds_ref[0, region]
    other_kind = kinds_ref[0, 1 - region]
    one = jnp.int32(1)
    own_variance = 0.5 * lax.shift_left(one, own_kind).astype(f32)
    other_variance = 0.5 * lax.shift_left(one, other_kind).astype(f32)
    cross_weight = jnp.where(groups_ref[0, 0] == groups_ref[0, 1], f32(TAPER_BASE), f32(0.0))
    count = total_members - 1

    seen[:tile, :] = own_ref[:, :total_members]
    seen[tile:, :] = other_ref[:, :total_members]
    in_own = lax.broadcasted_iota(jnp.int32, (rows, 1), 0) < tile
    variance = jnp.where(in_own, own_variance, other_variance)

    product = lax.dot_general(
        seen[...], seen[tile:, :], (((1,), (1,)), ((), ())), preferred_element_type=f32
    )
    covariance[:tile, :tile] = own_covariance_ref[...]
    between = product[:tile, :] * (cross_weight / count)
    covariance[:tile, tile:] = between.astype(bf16)
    covariance[tile:, :tile] = jnp.transpose(between).astype(bf16)
    covariance[tile:, tile:] = (product[tile:, :] * (f32(1.0) / count)).astype(bf16)
    bound = variance + jnp.sum(jnp.abs(covariance[...].astype(f32)), axis=1, keepdims=True)
    largest = jnp.max(bound)
    lowest = jnp.minimum(own_variance, other_variance)
    highest = lowest + largest
    center = 0.5 * (highest + lowest)
    radius = 0.5 * (highest - lowest)
    sigma = center / radius
    rho = 1.0 / sigma

    own_base = jnp.sum(own_ref[:, total_members:].astype(f32)[:, :3], axis=1, keepdims=True)
    other_base = jnp.sum(other_ref[:, total_members:].astype(f32)[:, :3], axis=1, keepdims=True)
    own_scale = jnp.sqrt(jnp.full((1, 1), own_variance, f32))
    other_scale = jnp.sqrt(jnp.full((1, 1), other_variance, f32))
    width = SOLVE_COLUMNS

    steps = []
    reach_before, keep_before = 1.0 / center, f32(0.0)
    for _ in range(ITERS - 1):
        rho_next = 1.0 / (2.0 * sigma - rho)
        keep = rho_next * rho
        reach = 2.0 * rho_next / radius
        ratio = reach / reach_before
        steps.append((keep + ratio - reach * variance, ratio * keep_before, reach))
        rho, reach_before, keep_before = rho_next, reach, keep
    inverse = 1.0 / center

    spans = [slice(left, left + width) for left in range(0, total_members, width)]
    devices, members, _ = out_ref.shape
    places = place_of(devices)

    def apply(held, span):
        return jnp.dot(
            covariance[...], held[:, span].astype(bf16), preferred_element_type=f32
        )

    def settle(span):
        ahead, back, reach = steps[2]
        solved[:, span] = (
            (1.0 + ahead) * two_steps[:, span]
            + (1.0 - back) * one_step[:, span]
            + zero[:, span]
            - reach * apply(two_steps, span)
        ).astype(bf16)

    def finish(span):
        part = lax.dot_general(
            solved[:, span], gain[...], (((0,), (0,)), ((), ())), preferred_element_type=f32
        ).astype(bf16)
        for device in range(span.start // members, span.stop // members):
            first = device * members - span.start
            out_ref[places[device]] = part[first : first + members]

    for span in spans:
        zero[:tile, span] = inverse * (
            own_base + own_scale * own_noise_ref[:, span].astype(f32) - own_ref[:, span].astype(f32)
        )
        zero[tile:, span] = inverse * (
            other_base
            + other_scale * other_noise_ref[:, span].astype(f32)
            - other_ref[:, span].astype(f32)
        )
    gain[:tile, :] = own_gain_ref[...]
    cross = jnp.dot(seen[tile:, :], anomaly_ref[...], preferred_element_type=f32)
    gain[tile:, :] = (cross * (cross_weight / count)).astype(bf16)
    for span in spans:
        ahead, _, reach = steps[0]
        one_step[:, span] = ahead * zero[:, span] - reach * apply(zero, span)
    for span in spans:
        ahead, back, reach = steps[1]
        two_steps[:, span] = (
            ahead * one_step[:, span] - back * zero[:, span] - reach * apply(one_step, span)
        )
    settle(spans[0])
    for span, later in zip(spans, spans[1:]):
        settle(later)
        finish(span)
    finish(spans[-1])


def shards(
    prior_samples, measured_point, measured_reading, measurement_noise, noise_kind, taper_set
):
    members, bands, _, cells = prior_samples.shape
    tile = measured_point.shape[2]
    total = measurement_noise.shape[3]
    chunks = cells // LANES
    width = cells + LANES
    swap = [(0, 1), (1, 0)]

    own_noise = measurement_noise.reshape(tile, total)

    packed = pl.pallas_call(
        pack_members,
        in_specs=[pl.BlockSpec(memory_space=pltpu.HBM)],
        out_specs=pl.BlockSpec(memory_space=pltpu.VMEM),
        out_shape=jax.ShapeDtypeStruct((bands, members, width), bf16),
        scratch_shapes=[
            pltpu.VMEM((members, bands, chunks, LANES), f32),
            pltpu.SemaphoreType.DMA((GROUPS,)),
        ],
        cost_estimate=pl.CostEstimate(
            flops=4 * members * bands * cells, bytes_accessed=7 * members * bands * cells, transcendentals=0
        ),
        compiler_params=pltpu.CompilerParams(vmem_limit_bytes=50 * MIB),
        name="pack_members",
    )(prior_samples.reshape(members, bands, chunks, LANES))

    arrived, own_noise = lax.optimization_barrier((exchange(packed), own_noise))
    other_noise = lax.ppermute(own_noise, "region", swap)

    anomaly, seen = pl.pallas_call(
        observe,
        in_specs=[pl.BlockSpec(memory_space=pltpu.VMEM)] * 3,
        out_specs=[pl.BlockSpec(memory_space=pltpu.VMEM)] * 2,
        out_shape=[
            jax.ShapeDtypeStruct((total, cells), bf16),
            jax.ShapeDtypeStruct((tile, total + LANES), bf16),
        ],
        scratch_shapes=[
            pltpu.VMEM((bands, chunks, LANES), f32),
            pltpu.VMEM((bands, chunks, LANES), f32),
            pltpu.VMEM((tile, cells), bf16),
        ],
        cost_estimate=pl.CostEstimate(
            flops=2 * tile * total * cells, bytes_accessed=8 * MIB, transcendentals=0
        ),
        compiler_params=pltpu.CompilerParams(vmem_limit_bytes=12 * MIB),
        name="observe",
    )(arrived, measured_point.reshape(1, tile), measured_reading.reshape(1, tile))

    seen, other_noise = lax.optimization_barrier((seen, other_noise))
    other_seen = lax.ppermute(seen, "region", swap)

    own_gain, own_covariance = pl.pallas_call(
        own_part,
        in_specs=[pl.BlockSpec(memory_space=pltpu.VMEM)] * 2,
        out_specs=[pl.BlockSpec(memory_space=pltpu.VMEM)] * 2,
        out_shape=[
            jax.ShapeDtypeStruct((tile, cells), bf16),
            jax.ShapeDtypeStruct((tile, tile), bf16),
        ],
        cost_estimate=pl.CostEstimate(
            flops=2 * tile * total * (cells + tile), bytes_accessed=8 * MIB, transcendentals=0
        ),
        compiler_params=pltpu.CompilerParams(vmem_limit_bytes=12 * MIB),
        name="own_part",
    )(anomaly, seen)

    increment = pl.pallas_call(
        analyse,
        in_specs=[pl.BlockSpec(memory_space=pltpu.SMEM)] * 2
        + [pl.BlockSpec(memory_space=pltpu.VMEM)] * 7,
        out_specs=pl.BlockSpec(memory_space=pltpu.VMEM),
        out_shape=jax.ShapeDtypeStruct((bands, members, cells), bf16),
        scratch_shapes=[
            pltpu.VMEM((2 * tile, total), bf16),
            pltpu.VMEM((2 * tile, 2 * tile), bf16),
            pltpu.VMEM((2 * tile, cells), bf16),
            pltpu.VMEM((2 * tile, total), bf16),
            pltpu.VMEM((2 * tile, total), f32),
            pltpu.VMEM((2 * tile, total), f32),
            pltpu.VMEM((2 * tile, total), f32),
        ],
        compiler_params=pltpu.CompilerParams(vmem_limit_bytes=28 * MIB),
        name="analyse",
    )(
        noise_kind,
        taper_set,
        anomaly,
        seen,
        own_gain,
        own_covariance,
        other_seen,
        own_noise,
        other_noise,
    )

    returned = exchange(increment)

    unpacked = pl.pallas_call(
        unpack_members,
        in_specs=[pl.BlockSpec(memory_space=pltpu.VMEM)],
        out_specs=pl.BlockSpec(memory_space=pltpu.HBM),
        out_shape=jax.ShapeDtypeStruct((members, bands, chunks, LANES), f32),
        scratch_shapes=[
            pltpu.VMEM((members, bands, chunks, LANES), f32),
            pltpu.SemaphoreType.DMA((GROUPS,)),
        ],
        compiler_params=pltpu.CompilerParams(vmem_limit_bytes=12 * MIB),
        name="unpack_members",
    )(returned)
    return unpacked.reshape(members, bands, 1, cells)


def solution(mesh):
    return jax.shard_map(
        shards,
        mesh=mesh,
        in_specs=(
            P("member", None, "region", None),
            P("member", "region", None),
            P("member", "region", None),
            P("member", "region", None, None),
            P("member", None),
            P("member", None),
        ),
        out_specs=P("member", None, "region", None),
        check_vma=False,
    )
```

```python
import jax
import jax.numpy as jnp
from jax import lax
from jax.experimental import pallas as pl
from jax.experimental.pallas import tpu as pltpu
from jax.sharding import PartitionSpec as P

ITERS = 4
TAPER_BASE = 0.7
LANES = 128
GROUPS = 8
COLUMNS = 512
SOLVE_COLUMNS = 256
MIB = 1024 * 1024

STRIDE = 21

f32 = jnp.float32
bf16 = jnp.bfloat16


def group_order(devices):
    return [STRIDE * place % devices for place in range(devices)]


def place_of(devices):
    places = [0] * devices
    for place, device in enumerate(group_order(devices)):
        places[device] = place
    return places


def exchange(value):
    order = group_order(value.shape[0])
    return lax.all_to_all(
        value, "member", split_axis=0, concat_axis=0, axis_index_groups=[order], tiled=True
    )


def split3(value):
    high = value.astype(bf16)
    rest = value - high.astype(f32)
    middle = rest.astype(bf16)
    low = (rest - middle.astype(f32)).astype(bf16)
    return high, middle, low


def row_order(rows, members, chunks):
    to = lax.broadcasted_iota(jnp.int32, (rows, rows), 0)
    source = lax.broadcasted_iota(jnp.int32, (rows, rows), 1)
    wanted = lax.rem(to, members) * chunks + lax.div(to, members)
    return jnp.where(source == wanted, 1.0, 0.0).astype(bf16)


def pack_members(x_ref, out_ref, held, arrived):
    members, bands, chunks, lanes = x_ref.shape
    cells = chunks * lanes
    rows = members * chunks
    groups = arrived.shape[0]
    per_group = bands // groups

    def fetch(group):
        span = pl.ds(group * per_group, per_group)
        return pltpu.make_async_copy(x_ref.at[:, span], held.at[:, span], arrived.at[group])

    for group in range(groups):
        fetch(group).start()
    order = row_order(rows, members, chunks)
    place = place_of(bands)
    for group in range(groups):
        fetch(group).wait()
        for pair in range(group * per_group // 2, (group + 1) * per_group // 2):
            parts = []
            for band in (2 * pair, 2 * pair + 1):
                values = held[:, band]
                mean = jnp.sum(values, axis=0) * (1.0 / members)
                high = mean.astype(bf16)
                low = (mean - high.astype(f32)).astype(bf16)
                middle = high.astype(f32) + low.astype(f32)
                out_ref[place[band], :, cells : cells + lanes] = jnp.concatenate([high, low], axis=0)
                parts.append((values - middle[None]).reshape(rows, lanes).astype(bf16))
            moved = jnp.dot(
                order, jnp.concatenate(parts, axis=1), preferred_element_type=f32
            ).astype(bf16)
            for index in range(2):
                for chunk in range(chunks):
                    out_ref[place[2 * pair + index], :, chunk * lanes : (chunk + 1) * lanes] = moved[
                        chunk * members : (chunk + 1) * members,
                        index * lanes : (index + 1) * lanes,
                    ]


def unpack_members(x_ref, out_ref, held, sent):
    bands, members, cells = x_ref.shape
    chunks = cells // LANES
    rows = members * chunks
    groups = sent.shape[0]
    per_group = bands // groups
    order = row_order(rows, chunks, members)
    place = place_of(bands)

    def put(group):
        span = pl.ds(group * per_group, per_group)
        return pltpu.make_async_copy(held.at[:, span], out_ref.at[:, span], sent.at[group])

    for group in range(groups):
        for pair in range(group * per_group // 2, (group + 1) * per_group // 2):
            parts = []
            for band in (2 * pair, 2 * pair + 1):
                parts.append(
                    jnp.concatenate(
                        [
                            x_ref[place[band], :, c * LANES : (c + 1) * LANES]
                            for c in range(chunks)
                        ], axis=0
                    )
                )
            moved = jnp.dot(order, jnp.concatenate(parts, axis=1), preferred_element_type=f32)
            for index in range(2):
                held[:, 2 * pair + index] = moved[
                    :, index * LANES : (index + 1) * LANES
                ].reshape(members, chunks, LANES)
        put(group).start()
    for group in range(groups):
        put(group).wait()


def observe(x_ref, points_ref, readings_ref, anomaly_ref, seen_ref, means, spread, hot):
    sources, members, width = x_ref.shape
    cells = anomaly_ref.shape[1]
    total_members = anomaly_ref.shape[0]
    chunks = cells // LANES
    obs = points_ref.shape[1]

    place = place_of(sources)
    for source in range(sources):
        tail = x_ref[place[source], :, cells:width].astype(f32)
        means[source] = tail[:chunks] + tail[chunks:]
    average = jnp.sum(means[...], axis=0) * (1.0 / sources)

    points = jnp.transpose(jnp.broadcast_to(points_ref[...], (LANES, obs)))
    lane = lax.broadcasted_iota(jnp.int32, (obs, LANES), 1)
    picked = jnp.zeros((obs, LANES), f32)
    for chunk in range(chunks):
        here = points == lane + chunk * LANES
        hot[:, chunk * LANES : (chunk + 1) * LANES] = jnp.where(here, 1.0, 0.0).astype(bf16)
        picked = picked + jnp.where(here, average[chunk : chunk + 1, :], 0.0)
    readings = jnp.transpose(jnp.broadcast_to(readings_ref[...], (LANES, obs)))
    base = readings - jnp.sum(picked, axis=1, keepdims=True)
    high, middle, low = split3(base)
    seen_ref[:, total_members : total_members + LANES] = jnp.where(
        lane == 0, high.astype(f32), jnp.where(lane == 1, middle.astype(f32), low.astype(f32))
    ).astype(bf16)

    spread[...] = means[...] - average[None]

    for source in range(sources):
        rows = slice(source * members, (source + 1) * members)
        shift = spread[source]
        for chunk in range(chunks):
            columns = slice(chunk * LANES, (chunk + 1) * LANES)
            anomaly_ref[rows, columns] = (
                x_ref[place[source], :, columns].astype(f32) + shift[chunk : chunk + 1, :]
            ).astype(bf16)
    for start in range(0, total_members, COLUMNS):
        span = slice(start, start + COLUMNS)
        seen_ref[:, span] = lax.dot_general(
            hot[...],
            anomaly_ref[span, :],
            (((1,), (1,)), ((), ())),
            preferred_element_type=f32,
        ).astype(bf16)


def own_part(anomaly_ref, own_ref, gain_ref, covariance_ref):
    total_members = anomaly_ref.shape[0]
    count = total_members - 1
    rows = own_ref[:, :total_members]
    cross = jnp.dot(rows, anomaly_ref[...], preferred_element_type=f32)
    gain_ref[...] = (cross * (f32(1.0) / count)).astype(bf16)
    product = lax.dot_general(rows, rows, (((1,), (1,)), ((), ())), preferred_element_type=f32)
    covariance_ref[...] = (product * (f32(1.0) / count)).astype(bf16)


def analyse(
    kinds_ref,
    groups_ref,
    anomaly_ref,
    own_ref,
    own_gain_ref,
    own_covariance_ref,
    other_ref,
    own_noise_ref,
    other_noise_ref,
    out_ref,
    seen,
    covariance,
    gain,
    solved,
    zero,
    one_step,
    two_steps,
):
    total_members, cells = anomaly_ref.shape
    tile = own_ref.shape[0]
    rows = 2 * tile
    region = lax.axis_index("region")
    own_kind = kinds_ref[0, region]
    other_kind = kinds_ref[0, 1 - region]
    one = jnp.int32(1)
    own_variance = 0.5 * lax.shift_left(one, own_kind).astype(f32)
    other_variance = 0.5 * lax.shift_left(one, other_kind).astype(f32)
    cross_weight = jnp.where(groups_ref[0, 0] == groups_ref[0, 1], f32(TAPER_BASE), f32(0.0))
    count = total_members - 1

    seen[:tile, :] = own_ref[:, :total_members]
    seen[tile:, :] = other_ref[:, :total_members]
    in_own = lax.broadcasted_iota(jnp.int32, (rows, 1), 0) < tile
    variance = jnp.where(in_own, own_variance, other_variance)

    product = lax.dot_general(
        seen[...], seen[tile:, :], (((1,), (1,)), ((), ())), preferred_element_type=f32
    )
    covariance[:tile, :tile] = own_covariance_ref[...]
    between = product[:tile, :] * (cross_weight / count)
    covariance[:tile, tile:] = between.astype(bf16)
    covariance[tile:, :tile] = jnp.transpose(between).astype(bf16)
    covariance[tile:, tile:] = (product[tile:, :] * (f32(1.0) / count)).astype(bf16)
    bound = variance + jnp.sum(jnp.abs(covariance[...].astype(f32)), axis=1, keepdims=True)
    largest = jnp.max(bound)
    lowest = jnp.minimum(own_variance, other_variance)
    highest = lowest + largest
    center = 0.5 * (highest + lowest)
    radius = 0.5 * (highest - lowest)
    sigma = center / radius
    rho = 1.0 / sigma

    own_base = jnp.sum(own_ref[:, total_members:].astype(f32)[:, :3], axis=1, keepdims=True)
    other_base = jnp.sum(other_ref[:, total_members:].astype(f32)[:, :3], axis=1, keepdims=True)
    own_scale = jnp.sqrt(jnp.full((1, 1), own_variance, f32))
    other_scale = jnp.sqrt(jnp.full((1, 1), other_variance, f32))
    width = SOLVE_COLUMNS

    steps = []
    reach_before, keep_before = 1.0 / center, f32(0.0)
    for _ in range(ITERS - 1):
        rho_next = 1.0 / (2.0 * sigma - rho)
        keep = rho_next * rho
        reach = 2.0 * rho_next / radius
        ratio = reach / reach_before
        steps.append((keep + ratio - reach * variance, ratio * keep_before, reach))
        rho, reach_before, keep_before = rho_next, reach, keep
    inverse = 1.0 / center

    spans = [slice(left, left + width) for left in range(0, total_members, width)]
    devices, members, _ = out_ref.shape
    places = place_of(devices)

    def apply(held, span):
        return jnp.dot(
            covariance[...], held[:, span].astype(bf16), preferred_element_type=f32
        )

    def settle(span):
        ahead, back, reach = steps[2]
        solved[:, span] = (
            (1.0 + ahead) * two_steps[:, span]
            + (1.0 - back) * one_step[:, span]
            + zero[:, span]
            - reach * apply(two_steps, span)
        ).astype(bf16)

    def finish(span):
        part = lax.dot_general(
            solved[:, span], gain[...], (((0,), (0,)), ((), ())), preferred_element_type=f32
        ).astype(bf16)
        for device in range(span.start // members, span.stop // members):
            first = device * members - span.start
            out_ref[places[device]] = part[first : first + members]

    for span in spans:
        zero[:tile, span] = inverse * (
            own_base + own_scale * own_noise_ref[:, span].astype(f32) - own_ref[:, span].astype(f32)
        )
        zero[tile:, span] = inverse * (
            other_base
            + other_scale * other_noise_ref[:, span].astype(f32)
            - other_ref[:, span].astype(f32)
        )
    gain[:tile, :] = own_gain_ref[...]
    cross = jnp.dot(seen[tile:, :], anomaly_ref[...], preferred_element_type=f32)
    gain[tile:, :] = (cross * (cross_weight / count)).astype(bf16)
    for span in spans:
        ahead, _, reach = steps[0]
        one_step[:, span] = ahead * zero[:, span] - reach * apply(zero, span)
    for span in spans:
        ahead, back, reach = steps[1]
        two_steps[:, span] = (
            ahead * one_step[:, span] - back * zero[:, span] - reach * apply(one_step, span)
        )
    settle(spans[0])
    for span, later in zip(spans, spans[1:]):
        settle(later)
        finish(span)
    finish(spans[-1])


def shards(
    prior_samples, measured_point, measured_reading, measurement_noise, noise_kind, taper_set
):
    members, bands, _, cells = prior_samples.shape
    tile = measured_point.shape[2]
    total = measurement_noise.shape[3]
    chunks = cells // LANES
    width = cells + LANES
    swap = [(0, 1), (1, 0)]

    own_noise = measurement_noise.reshape(tile, total)

    packed = pl.pallas_call(
        pack_members,
        in_specs=[pl.BlockSpec(memory_space=pltpu.HBM)],
        out_specs=pl.BlockSpec(memory_space=pltpu.VMEM),
        out_shape=jax.ShapeDtypeStruct((bands, members, width), bf16),
        scratch_shapes=[
            pltpu.VMEM((members, bands, chunks, LANES), f32),
            pltpu.SemaphoreType.DMA((GROUPS,)),
        ],
        cost_estimate=pl.CostEstimate(
            flops=4 * members * bands * cells, bytes_accessed=7 * members * bands * cells, transcendentals=0
        ),
        compiler_params=pltpu.CompilerParams(vmem_limit_bytes=50 * MIB),
        name="pack_members",
    )(prior_samples.reshape(members, bands, chunks, LANES))

    arrived, own_noise = lax.optimization_barrier((exchange(packed), own_noise))
    other_noise = lax.ppermute(own_noise, "region", swap)

    anomaly, seen = pl.pallas_call(
        observe,
        in_specs=[pl.BlockSpec(memory_space=pltpu.VMEM)] * 3,
        out_specs=[pl.BlockSpec(memory_space=pltpu.VMEM)] * 2,
        out_shape=[
            jax.ShapeDtypeStruct((total, cells), bf16),
            jax.ShapeDtypeStruct((tile, total + LANES), bf16),
        ],
        scratch_shapes=[
            pltpu.VMEM((bands, chunks, LANES), f32),
            pltpu.VMEM((bands, chunks, LANES), f32),
            pltpu.VMEM((tile, cells), bf16),
        ],
        cost_estimate=pl.CostEstimate(
            flops=2 * tile * total * cells, bytes_accessed=8 * MIB, transcendentals=0
        ),
        compiler_params=pltpu.CompilerParams(vmem_limit_bytes=12 * MIB),
        name="observe",
    )(arrived, measured_point.reshape(1, tile), measured_reading.reshape(1, tile))

    other_seen = lax.ppermute(seen, "region", swap)

    own_gain, own_covariance = pl.pallas_call(
        own_part,
        in_specs=[pl.BlockSpec(memory_space=pltpu.VMEM)] * 2,
        out_specs=[pl.BlockSpec(memory_space=pltpu.VMEM)] * 2,
        out_shape=[
            jax.ShapeDtypeStruct((tile, cells), bf16),
            jax.ShapeDtypeStruct((tile, tile), bf16),
        ],
        cost_estimate=pl.CostEstimate(
            flops=2 * tile * total * (cells + tile), bytes_accessed=8 * MIB, transcendentals=0
        ),
        compiler_params=pltpu.CompilerParams(vmem_limit_bytes=12 * MIB),
        name="own_part",
    )(anomaly, seen)

    increment = pl.pallas_call(
        analyse,
        in_specs=[pl.BlockSpec(memory_space=pltpu.SMEM)] * 2
        + [pl.BlockSpec(memory_space=pltpu.VMEM)] * 7,
        out_specs=pl.BlockSpec(memory_space=pltpu.VMEM),
        out_shape=jax.ShapeDtypeStruct((bands, members, cells), bf16),
        scratch_shapes=[
            pltpu.VMEM((2 * tile, total), bf16),
            pltpu.VMEM((2 * tile, 2 * tile), bf16),
            pltpu.VMEM((2 * tile, cells), bf16),
            pltpu.VMEM((2 * tile, total), bf16),
            pltpu.VMEM((2 * tile, total), f32),
            pltpu.VMEM((2 * tile, total), f32),
            pltpu.VMEM((2 * tile, total), f32),
        ],
        compiler_params=pltpu.CompilerParams(vmem_limit_bytes=28 * MIB),
        name="analyse",
    )(
        noise_kind,
        taper_set,
        anomaly,
        seen,
        own_gain,
        own_covariance,
        other_seen,
        own_noise,
        other_noise,
    )

    returned = exchange(increment)

    unpacked = pl.pallas_call(
        unpack_members,
        in_specs=[pl.BlockSpec(memory_space=pltpu.VMEM)],
        out_specs=pl.BlockSpec(memory_space=pltpu.HBM),
        out_shape=jax.ShapeDtypeStruct((members, bands, chunks, LANES), f32),
        scratch_shapes=[
            pltpu.VMEM((members, bands, chunks, LANES), f32),
            pltpu.SemaphoreType.DMA((GROUPS,)),
        ],
        compiler_params=pltpu.CompilerParams(vmem_limit_bytes=12 * MIB),
        name="unpack_members",
    )(returned)
    return unpacked.reshape(members, bands, 1, cells)


def solution(mesh):
    return jax.shard_map(
        shards,
        mesh=mesh,
        in_specs=(
            P("member", None, "region", None),
            P("member", "region", None),
            P("member", "region", None),
            P("member", "region", None, None),
            P("member", None),
            P("member", None),
        ),
        out_specs=P("member", None, "region", None),
        check_vma=False,
    )
```
